256 devices in a mesh: grp: 16 (over x_hi, y, core), blk: 16 (over x_lo, z).
Axes of the slice: x: 4 (x_hi: 2, x_lo: 2; x = x_hi * 2 + x_lo), y: 4, z: 8, core: 2. Of those that a mesh axis runs over, the one named last changes fastest.
Arguments:
- factors: float32 [1024, 24, 8192], P('grp', None, 'blk'), may hold values from -0.078125 to 0.078125
Outputs:
- exchange_pairs: float32 [9, 512, 16, 512], P(None, 'grp', 'blk')
The draws below stay inside these ranges and needn't reach their ends.
All inputs are finite; a program needn't handle non-finite values.
Results may differ from the reference program's by a relative error of at most 0.00012.
Values sent between devices are 32-bit elements; how exact they have to be, the bound alone decides.
A program may use at most 256 MiB of HBM per device.

```python
import jax
import jax.numpy as jnp
from jax import lax

AUX_GRP = 64
OCC = 24
NB_DEV = 512
AUXILIARIES = 1024
N = 8192
HALF = 9
N_BLK = 16


def block_scale(stream_key, shape, cuts, least, high):
    level = 1.0
    for position, shards_of in cuts:
        steps = jax.random.uniform(jax.random.fold_in(jax.random.fold_in(stream_key, 6), position), (shards_of,), jnp.float32, least / len(cuts), high / len(cuts))
        level = level * jnp.repeat(jnp.exp(steps), shape[position] // shards_of).reshape((-1,) + (1,) * (len(shape) - 1 - position))
    return level


def scatter_about(rng, dims, deviation, reach, shards=(), dtype=jnp.bfloat16):
    result = deviation * jax.random.normal(rng, dims, jnp.float32)
    if shards:
        result = result * block_scale(rng, dims, shards, -0.22, 0.18)
    return jnp.clip(result, -reach, reach).astype(dtype)


def setup_inputs(seed: int = 0) -> dict:
    key_of = jax.random.split(jax.random.key(seed), 2)
    factors = scatter_about(key_of[0], (AUXILIARIES, OCC, N), (4 * AUX_GRP * OCC) ** -0.5, 0.078125, ((0, 16), (2, 16)), jnp.float32)
    return {"factors": factors}


def reference(factors):
    blocks = factors.reshape(AUXILIARIES, OCC, N_BLK, NB_DEV)
    pieces = []
    for distance in range(HALF):
        rolled = jnp.roll(blocks, -distance, axis=2)
        pieces.append(jnp.einsum("picr,pics->rcs", rolled, blocks, precision=lax.Precision.HIGHEST))
    return jnp.stack(pieces, axis=0)
```

```python
import jax
import jax.numpy as jnp
from jax import lax
from jax.experimental import pallas as pl
from jax.experimental.pallas import tpu as pltpu
from jax.sharding import PartitionSpec as P

MESH = pl.DeviceIdType.MESH
OWN, P1, M1, Q1, M2, P2, Q2 = range(7)
OFFSET = {OWN: (0, 0), P1: (0, 1), M1: (0, -1), Q1: (1, 1), M2: (0, -2), P2: (0, 2), Q2: (1, 2)}
PAIRS = [(OWN, OWN), (P1, OWN), (P1, M1), (Q1, P1), (Q1, OWN), (Q1, M1), (M2, P1), (M2, Q1), (M2, P2), (M2, Q2)]
BATCHES = [(0, 12), (12, 12), (24, 6), (30, 10)]
TILES = 40


def kernel(x, out, f32, q2, own, hi, lo, prod, core_in, y_in, fin,
           link_send, link_recv, own_sem, core_send, core_recv, y_send, y_recv, fin_send, fin_recv):
    grp, blk = lax.axis_index("grp"), lax.axis_index("blk")
    core, y, h = lax.rem(grp, 2), lax.rem(lax.div(grp, 2), 4), lax.div(grp, 8)
    z, row = lax.rem(blk, 8), lax.div(blk, 8)
    part = f32.shape[2] // 2

    def at_blk(dl, dz):
        return lax.rem(row + dl, 2) * 8 + lax.rem(z + dz + 8, 8)

    def at_grp(dh, dy, dk):
        return lax.rem(h + dh, 2) * 8 + lax.rem(y + dy, 4) * 2 + lax.rem(core + dk, 2)

    greet = [(grp, at_blk(1, 0)), (at_grp(0, 0, 1), blk)]
    greet += [(at_grp(0, dy, 0), blk) for dy in (1, 2, 3)]
    plane = [(0, 0), (0, 1), (0, -1), (0, 2), (0, -2), (1, 1), (1, -1), (1, 2), (1, -2)]
    for dh in range(2):
        greet += [(at_grp(dh, 0, 0), at_blk(dl, dz)) for dl, dz in plane if (dh, dl, dz) != (0, 0, 0)]
    barrier = pltpu.get_barrier_semaphore()
    for dev in greet:
        pl.semaphore_signal(barrier, inc=1, device_id=dev, device_id_type=MESH)
    pl.semaphore_wait(barrier, len(greet))

    down, up, across = (grp, at_blk(0, -1)), (grp, at_blk(0, 1)), (grp, at_blk(1, 0))

    def half_of(step):
        return lax.rem(1 - row + step, 2)

    def window(buf, half, step):
        return buf.at[half, pl.ds(half_of(step) * part, part)]

    def link(stream, half, step):
        slot = (P1, M1, P2, M2, Q1, Q2)[stream]
        dev = (down, up, down, up, across, across)[stream]
        sem = stream * 4 + half * 2 + step
        if stream < 2:
            src = x.at[pl.ds(half_of(step) * part, part), :, pl.ds(half * 256, 256)]
        else:
            src = window(f32.at[(P1, M1, P1, P2)[stream - 2] - 1], half, step)
        dst = q2.at[half] if slot == Q2 else window(f32.at[slot - 1], half, step)
        return pltpu.make_async_remote_copy(src_ref=src, dst_ref=dst, send_sem=link_send.at[sem],
                                            recv_sem=link_recv.at[sem], device_id=dev, device_id_type=MESH)

    pieces = [(half, step) for half in range(2) for step in range(2)]
    for half, step in pieces:
        link(0, half, step).start()
        link(1, half, step).start()

    def split(a, slot, half, kh):
        a = a.reshape(-1, 256)
        top = a.astype(jnp.bfloat16)
        hi[slot, half, kh] = top
        lo[slot, half, kh] = (a - top.astype(jnp.float32)).astype(jnp.bfloat16)

    def split_slot(slot, half):
        @pl.loop(0, 2)
        def _(kh):
            split(f32[slot - 1, half, pl.ds(kh * part, part)], slot, half, kh)

    @pl.loop(0, 4)
    def _(i):
        half, kh = lax.div(i, 2), lax.rem(i, 2)
        copy = pltpu.make_async_copy(
            x.at[pl.ds(kh * part, part), :, pl.ds(pl.multiple_of(half * 256, 256), 256)], own, own_sem)
        copy.start()
        copy.wait()
        split(own[...], OWN, half, kh)

    meta = []
    for s, t in PAIRS:
        i, j = at_blk(*OFFSET[s]), at_blk(*OFFSET[t])
        diff = lax.rem(i - j + 16, 16)
        straight = diff <= 8
        meta.append((straight, jnp.where(straight, s, t), jnp.where(straight, t, s),
                     jnp.where(straight, j, i), jnp.where(straight, diff, 16 - diff)))
    share = {8: lax.div(z, 4), 9: row}

    def tile(pair, a, b, pos):
        _, rows, cols, _, _ = meta[pair]
        dims = (((0,), (0,)), ((), ()))
        total = None
        for kh in ([share[pair]] if pair in share else [0, 1]):
            for left, right in ((hi, hi), (hi, lo), (lo, hi)):
                term = lax.dot_general(left[rows, a, kh], right[cols, b, kh], dims,
                                       preferred_element_type=jnp.float32)
                total = term if total is None else total + term
        total = total.reshape(4, 2, 32, 256)
        prod[0, pos] = total[:, 0]
        prod[1, pos] = total[:, 1]

    def place(pair, i, j):
        straight = meta[pair][0]
        return jnp.where(straight, i, j), jnp.where(straight, j, i)

    def whole_pair(pair):
        @pl.loop(0, 4)
        def _(q):
            tile(pair, lax.div(q, 2), lax.rem(q, 2), pair * 4 + q)

    def late(pair, half):
        if pair < 8:
            return 2, lambda t: (half, t)
        if half == 0:
            return 1, lambda t: (0, 0)
        return 3, lambda t: (lax.div(t + 1, 2), lax.rem(t + 1, 2))

    first = {}
    pos = 24
    for half in range(2):
        for pair in (6, 7, 8, 9):
            first[pair, half] = pos
            pos += late(pair, half)[0]

    def late_pair(pair, half):
        count, halves = late(pair, half)

        @pl.loop(0, count)
        def _(t):
            a, b = place(pair, *halves(t))
            tile(pair, a, b, first[pair, half] + t)

    def core_copy(batch):
        start, n = BATCHES[batch]
        return pltpu.make_async_remote_copy(
            src_ref=prod.at[1 - core, pl.ds(start, n)], dst_ref=core_in.at[pl.ds(start, n)],
            send_sem=core_send.at[batch], recv_sem=core_recv.at[batch],
            device_id=(at_grp(0, 0, 1), blk), device_id_type=MESH)

    def y_copy(batch, dy):
        start, n = BATCHES[batch]
        return pltpu.make_async_remote_copy(
            src_ref=prod.at[core, pl.ds(start, n), lax.rem(y + dy, 4)], dst_ref=y_in.at[dy - 1, pl.ds(start, n)],
            send_sem=y_send.at[batch * 3 + dy - 1], recv_sem=y_recv.at[batch * 3 + dy - 1],
            device_id=(at_grp(0, dy, 0), blk), device_id_type=MESH)

    def core_finish(batch):
        start, n = BATCHES[batch]
        core_copy(batch).wait()

        @pl.loop(start, start + n)
        def _(q):
            prod[core, q] = prod[core, q] + core_in[q]

        for dy in (1, 2, 3):
            y_copy(batch, dy).start()

    def fin_copy(pair, a, b, pos, wait):
        _, _, _, owner, distance = meta[pair]
        slot = distance + 5 * share[pair] if pair in share else distance
        mine = jnp.logical_and(a == h, owner == blk)
        src, dst, sem = prod.at[core, pos, y], fin.at[slot, h, b], fin_recv.at[slot * 4 + h * 2 + b]
        if not wait:
            @pl.when(mine)
            def _():
                pltpu.make_async_copy(src, dst, sem).start()

        @pl.when(jnp.logical_not(mine))
        def _():
            copy = pltpu.make_async_remote_copy(
                src_ref=src, dst_ref=dst, send_sem=fin_send.at[pos], recv_sem=sem,
                device_id=(a * 8 + y * 2 + core, owner), device_id_type=MESH)
            if wait:
                copy.wait_send()
            else:
                copy.start()

    def fin_batch(batch, wait):
        if batch < 2:
            for pair in range(3 * batch, 3 * batch + 3):
                @pl.loop(0, 4)
                def _(q, pair=pair):
                    fin_copy(pair, lax.div(q, 2), lax.rem(q, 2), pair * 4 + q, wait)
        else:
            for pair in (6, 7, 8, 9):
                count, halves = late(pair, batch - 2)

                @pl.loop(0, count)
                def _(t, pair=pair, halves=halves):
                    a, b = place(pair, *halves(t))
                    fin_copy(pair, a, b, first[pair, batch - 2] + t, wait)

    def y_finish(batch):
        start, n = BATCHES[batch]
        for dy in (1, 2, 3):
            y_copy(batch, dy).wait()

        @pl.loop(start, start + n)
        def _(q):
            prod[core, q, y] = (prod[core, q, y] + y_in[0, q]) + (y_in[1, q] + y_in[2, q])

        fin_batch(batch, False)

    whole_pair(0)
    for half, step in pieces:
        link(0, half, step).wait_recv()
        link(2, half, step).start()
        link(4, half, step).start()
        link(1, half, step).wait_recv()
        link(3, half, step).start()
    for half in range(2):
        split_slot(P1, half)
        split_slot(M1, half)
    whole_pair(1)
    whole_pair(2)
    core_copy(0).start()
    for half, step in pieces:
        link(4, half, step).wait_recv()
    link(2, 0, 0).wait_recv()
    link(5, 0, 0).start()
    for half in range(2):
        split_slot(Q1, half)
    for pair in (3, 4, 5):
        whole_pair(pair)
    core_copy(1).start()
    core_finish(0)
    core_finish(1)
    y_finish(0)

    for half in range(2):
        if half == 1:
            link(2, 1, 0).wait_recv()
            link(5, 1, 0).start()
            core_finish(2)
            y_finish(1)
        link(3, half, 0).wait_recv()
        link(3, half, 1).wait_recv()
        split_slot(M2, half)
        late_pair(6, half)
        late_pair(7, half)
        if half == 1:
            y_finish(2)
        link(2, half, 1).wait_recv()
        split_slot(P2, half)
        late_pair(8, half)
        link(5, half, 0).wait_recv()
        split(q2[half], Q2, half, row)
        late_pair(9, half)
        core_copy(2 + half).start()
    core_finish(3)
    y_finish(3)

    for d in [0, 1, 2, 3, 5, 6, 7, 8, 4]:
        slots = [d, 9] if d == 4 else [d]
        for b in range(2):
            for slot in slots:
                for src in range(2):
                    pltpu.make_async_copy(fin.at[slot, src, b], fin.at[slot, src, b],
                                          fin_recv.at[slot * 4 + src * 2 + b]).wait()
            total = fin[d, 0, b] + fin[d, 1, b]
            if d == 4:
                total = total + (fin[9, 0, b] + fin[9, 1, b])
            out[d, :, b * 256:(b + 1) * 256] = total

    for half, step in pieces:
        for stream in range(6 if step == 0 else 5):
            link(stream, half, step).wait_send()
    for batch in range(4):
        fin_batch(batch, True)


def per_device(factors):
    aux, orbitals, width = factors.shape
    part = aux // 2
    depth = part * orbitals
    dma = pltpu.SemaphoreType.DMA
    out = pl.pallas_call(
        kernel,
        out_shape=jax.ShapeDtypeStruct((9, 32, width), jnp.float32),
        in_specs=[pl.BlockSpec(memory_space=pl.ANY)],
        out_specs=pl.BlockSpec(memory_space=pltpu.VMEM),
        scratch_shapes=[
            pltpu.VMEM((5, 2, aux, orbitals, 256), jnp.float32),
            pltpu.VMEM((2, part, orbitals, 256), jnp.float32),
            pltpu.VMEM((part, orbitals, 256), jnp.float32),
            pltpu.VMEM((7, 2, 2, depth, 256), jnp.bfloat16),
            pltpu.VMEM((7, 2, 2, depth, 256), jnp.bfloat16),
            pltpu.VMEM((2, TILES, 4, 32, 256), jnp.float32),
            pltpu.VMEM((TILES, 4, 32, 256), jnp.float32),
            pltpu.VMEM((3, TILES, 32, 256), jnp.float32),
            pltpu.VMEM((10, 2, 2, 32, 256), jnp.float32),
            dma((24,)), dma((24,)), dma, dma((4,)), dma((4,)), dma((12,)), dma((12,)), dma((TILES,)), dma((40,)),
        ],
        compiler_params=pltpu.CompilerParams(
            collective_id=0, has_side_effects=True, vmem_limit_bytes=62 * 2**20),
        cost_estimate=pl.CostEstimate(flops=6 * 9 * 512 * 512 * aux * orbitals, bytes_accessed=4 * 2**20,
                                      transcendentals=0),
        name="exchange",
    )(factors)
    return out[:, :, None, :]


def solution(mesh):
    return jax.shard_map(
        per_device,
        mesh=mesh,
        in_specs=(P("grp", None, "blk"),),
        out_specs=P(None, "grp", "blk", None),
        check_vma=False,
    )
```

```python
import jax
import jax.numpy as jnp
from jax import lax
from jax.experimental import pallas as pl
from jax.experimental.pallas import tpu as pltpu
from jax.sharding import PartitionSpec as P

MESH = pl.DeviceIdType.MESH
OWN, P1, M1, Q1, M2, P2, Q2 = range(7)
OFFSET = [(0, 0), (0, 1), (0, -1), (1, 1), (0, -2), (0, 2), (1, 2)]
ORDER = [0, 3, 5, 2, 7, 1, 4, 6]
N_M2, N_P2 = 5, 4


def pairs(s, t, halves):
    return [(s, i, t, j) for i, j in halves]


ALL = [(0, 0), (0, 1), (1, 0), (1, 1)]
A, B = [(0, 0), (0, 1)], [(1, 0), (1, 1)]
BATCHES = [
    [(8, pairs(OWN, OWN, ALL))],
    [(8, pairs(P1, OWN, A) + pairs(P1, M1, ALL[:1])), (8, pairs(Q1, OWN, A) + pairs(Q1, P1, ALL[:1]) + pairs(Q1, M1, ALL[:1]))],
    [(8, pairs(P1, OWN, B) + pairs(P1, M1, ALL[1:]) + pairs(Q1, P1, ALL[1:2]) + pairs(Q1, M1, ALL[1:2]))],
    [(8, pairs(Q1, OWN, B) + pairs(Q1, P1, B) + pairs(Q1, M1, B))],
    [(5, pairs(M2, P1, A) + pairs(M2, Q1, A)), (3, pairs(P2, M1, A) + pairs(Q2, M1, A)),
     (4, pairs(M2, P2, ALL[:1]) + pairs(M2, Q2, ALL[:1]))],
    [(3, pairs(P2, M1, B) + pairs(Q2, M1, B)), (4, pairs(M2, P2, ALL[1:2]) + pairs(M2, Q2, ALL[1:2]))],
    [(5, pairs(M2, P1, B) + pairs(M2, Q1, B)), (4, pairs(M2, P2, B) + pairs(M2, Q2, B))],
]
FIRST, COUNT = [], []
for batch in BATCHES:
    FIRST.append(sum(COUNT))
    COUNT.append(sum(len(tiles) for _, tiles in batch))
TILES = sum(COUNT)


def pick(t, values):
    out = values[0]
    for k in range(1, len(values)):
        if values[k] != values[k - 1]:
            out = jnp.where(t >= k, values[k], out)
    return out


def kernel(x, out, near, m2, p2, q2, own, hi, lo, prod, core_in, y_in, fin,
           link_send, link_recv, own_sem, core_send, core_recv, y_send, y_recv, fin_send, fin_recv):
    grp, blk = lax.axis_index("grp"), lax.axis_index("blk")
    core, y, h = lax.rem(grp, 2), lax.rem(lax.div(grp, 2), 4), lax.div(grp, 8)
    z, row = lax.rem(blk, 8), lax.div(blk, 8)
    chunk = near.shape[2] // 8
    piece = near.shape[2] // 4

    def at_blk(dl, dz):
        return lax.rem(row + dl, 2) * 8 + lax.rem(z + dz + 8, 8)

    def at_grp(dh, dy, dk):
        return lax.rem(h + dh, 2) * 8 + lax.rem(y + dy, 4) * 2 + lax.rem(core + dk, 2)

    greet = [(grp, at_blk(1, 0)), (at_grp(0, 0, 1), blk)]
    greet += [(at_grp(0, dy, 0), blk) for dy in (1, 2, 3)]
    plane = [(0, 0), (0, 1), (0, -1), (0, 2), (0, -2), (1, 1), (1, -1), (1, 2), (1, -2)]
    for dh in range(2):
        greet += [(at_grp(dh, 0, 0), at_blk(dl, dz)) for dl, dz in plane if (dh, dl, dz) != (0, 0, 0)]
    barrier = pltpu.get_barrier_semaphore()
    for dev in greet:
        pl.semaphore_signal(barrier, inc=1, device_id=dev, device_id_type=MESH)
    pl.semaphore_wait(barrier, len(greet))

    down, up, across = (grp, at_blk(0, -1)), (grp, at_blk(0, 1)), (grp, at_blk(1, 0))

    def remote(src, dst, sem, dev):
        return pltpu.make_async_remote_copy(src_ref=src, dst_ref=dst, send_sem=link_send.at[sem],
                                            recv_sem=link_recv.at[sem], device_id=dev, device_id_type=MESH)

    def link(slot, half, i):
        if slot in (P1, M1, Q1):
            span = pl.ds(i * piece, piece)
            src = near.at[P1 - 1, half, span] if slot == Q1 else x.at[span, :, pl.ds(half * 256, 256)]
            return remote(src, near.at[slot - 1, half, span], (slot - 1) * 8 + half * 4 + i,
                          {P1: down, M1: up, Q1: across}[slot])
        if slot == Q2:
            return remote(p2.at[half, i], q2.at[half, i], 42 + half * N_P2 + i, across)
        their_z = z + 1 if slot == M2 else z + 7
        span = pl.ds(lax.rem(their_z + 8 - ORDER[i], 8) * chunk, chunk)
        if slot == M2:
            return remote(near.at[M1 - 1, half, span], m2.at[half, i], 24 + half * N_M2 + i, up)
        return remote(near.at[P1 - 1, half, span], p2.at[half, i], 34 + half * N_P2 + i, down)

    for half in range(2):
        for i in range(4):
            link(P1, half, i).start()
            link(M1, half, i).start()

    def split(a, slot, half, p):
        a = a.reshape(-1, 256)
        top = a.astype(jnp.bfloat16)
        hi[slot, half, p] = top
        lo[slot, half, p] = (a - top.astype(jnp.float32)).astype(jnp.bfloat16)

    def span_at(p):
        return pl.ds(lax.rem(z + 8 - pick(p, ORDER), 8) * chunk, chunk)

    def split_near(slot, half):
        @pl.loop(0, 8)
        def _(p):
            split(near[slot - 1, half, span_at(p)], slot, half, p)

    def split_far(slot, half):
        src, n, keep, base = {M2: (m2, N_M2, M2, 0), P2: (p2, N_P2, P2, 0), Q2: (q2, N_P2, P2, N_P2)}[slot]

        @pl.loop(0, n)
        def _(p):
            split(src[half, p], keep, half, base + p)

    for half in range(2):
        copy = pltpu.make_async_copy(x.at[:, :, pl.ds(half * 256, 256)], own, own_sem)
        copy.start()
        copy.wait()

        @pl.loop(0, 8)
        def _(p):
            split(own[span_at(p)], OWN, half, p)

    def where_is(slot):
        return at_blk(pick(slot, [dl for dl, _ in OFFSET]), pick(slot, [dz for _, dz in OFFSET]))

    def tile_at(tiles, t):
        s, i, u, j = (pick(t, list(field)) for field in zip(*tiles))
        one, two = where_is(s), where_is(u)
        diff = lax.rem(one - two + 16, 16)
        straight = diff <= 8
        pick2 = lambda p, q: jnp.where(straight, p, q)
        return (pick2(s, u), pick2(i, j), pick2(u, s), pick2(j, i), pick2(two, one), pick2(diff, 16 - diff))

    def multiply(batch, group):
        chunks, tiles = BATCHES[batch][group]
        start = FIRST[batch] + sum(len(g) for _, g in BATCHES[batch][:group])

        @pl.loop(0, len(tiles))
        def _(t):
            rows, a, cols, b, _, _ = tile_at(tiles, t)

            def load(buf, slot, half):
                base = 0 if chunks == 8 else jnp.where(slot == Q2, N_P2, 0)
                kept = slot if chunks == 8 else jnp.where(slot == Q2, P2, slot)
                return buf[kept, half, pl.ds(base, chunks)].reshape(-1, 256)

            total = None
            for left, right in ((hi, hi), (hi, lo), (lo, hi)):
                term = lax.dot_general(load(left, rows, a), load(right, cols, b), (((0,), (0,)), ((), ())),
                                       preferred_element_type=jnp.float32)
                total = term if total is None else total + term
            total = total.reshape(4, 2, 32, 256)
            prod[0, start + t] = total[:, 0]
            prod[1, start + t] = total[:, 1]

    def core_copy(batch):
        span = pl.ds(FIRST[batch], COUNT[batch])
        return pltpu.make_async_remote_copy(
            src_ref=prod.at[1 - core, span], dst_ref=core_in.at[span],
            send_sem=core_send.at[batch], recv_sem=core_recv.at[batch],
            device_id=(at_grp(0, 0, 1), blk), device_id_type=MESH)

    def y_copy(batch, dy):
        span = pl.ds(FIRST[batch], COUNT[batch])
        return pltpu.make_async_remote_copy(
            src_ref=prod.at[core, span, lax.rem(y + dy, 4)], dst_ref=y_in.at[dy - 1, span],
            send_sem=y_send.at[batch * 3 + dy - 1], recv_sem=y_recv.at[batch * 3 + dy - 1],
            device_id=(at_grp(0, dy, 0), blk), device_id_type=MESH)

    def core_finish(batch):
        core_copy(batch).wait()

        @pl.loop(FIRST[batch], FIRST[batch] + COUNT[batch])
        def _(q):
            prod[core, q] = prod[core, q] + core_in[q]

        for dy in (1, 2, 3):
            y_copy(batch, dy).start()

    def y_finish(batch):
        for dy in (1, 2, 3):
            y_copy(batch, dy).wait()

        @pl.loop(FIRST[batch], FIRST[batch] + COUNT[batch])
        def _(q):
            prod[core, q, y] = (prod[core, q, y] + y_in[0, q]) + (y_in[1, q] + y_in[2, q])

    def deliver(batch, wait=False):
        start = FIRST[batch]
        for chunks, tiles in BATCHES[batch]:
            @pl.loop(0, len(tiles))
            def _(t, chunks=chunks, tiles=tiles, start=start):
                _, a, _, b, owner, distance = tile_at(tiles, t)
                place = {8: 0, 5: 0, 3: 1, 4: lax.div(z, 4)}[chunks]
                slot = distance + 6 * place
                src, sem = prod.at[core, start + t, y], slot * 4 + h * 2 + b
                mine = jnp.logical_and(a == h, owner == blk)
                if not wait:
                    @pl.when(mine)
                    def _():
                        pltpu.make_async_copy(src, fin.at[slot, h, b], fin_recv.at[sem]).start()

                @pl.when(jnp.logical_not(mine))
                def _():
                    copy = pltpu.make_async_remote_copy(
                        src_ref=src, dst_ref=fin.at[slot, h, b], send_sem=fin_send.at[start + t],
                        recv_sem=fin_recv.at[sem], device_id=(a * 8 + y * 2 + core, owner), device_id_type=MESH)
                    if wait:
                        copy.wait_send()
                    else:
                        copy.start()
            start += len(tiles)

    multiply(0, 0)
    core_copy(0).start()
    for i in range(4):
        link(P1, 0, i).wait_recv()
        link(Q1, 0, i).start()
    for i in range(4):
        link(M1, 0, i).wait_recv()
    for i in range(N_M2):
        if i < N_P2:
            link(P2, 0, i).start()
        link(M2, 0, i).start()
    core_finish(0)
    split_near(P1, 0)
    split_near(M1, 0)
    multiply(1, 0)
    link(P1, 1, 0).wait_recv()
    link(Q1, 1, 0).start()
    for i in range(4):
        link(Q1, 0, i).wait_recv()
    split_near(Q1, 0)
    multiply(1, 1)
    core_copy(1).start()
    link(P1, 1, 1).wait_recv()
    link(Q1, 1, 1).start()
    y_finish(0)
    core_finish(1)
    for i in (2, 3):
        link(P1, 1, i).wait_recv()
        link(Q1, 1, i).start()
    for i in range(4):
        link(M1, 1, i).wait_recv()
    for i in range(N_M2):
        if i < N_P2:
            link(P2, 1, i).start()
        link(M2, 1, i).start()
    split_near(P1, 1)
    split_near(M1, 1)
    multiply(2, 0)
    core_copy(2).start()
    for i in (0, 1):
        link(P2, 0, i).wait_recv()
        link(Q2, 0, i).start()
    for i in range(4):
        link(Q1, 1, i).wait_recv()
    split_near(Q1, 1)
    multiply(3, 0)
    core_copy(3).start()
    y_finish(1)
    for i in (2, 3):
        link(P2, 0, i).wait_recv()
        link(Q2, 0, i).start()
    core_finish(2)
    split_far(P2, 0)
    core_finish(3)
    for i in range(N_M2):
        link(M2, 0, i).wait_recv()
    split_far(M2, 0)
    multiply(4, 0)
    for i in range(N_P2):
        link(Q2, 0, i).wait_recv()
    link(P2, 1, 0).wait_recv()
    link(Q2, 1, 0).start()
    split_far(Q2, 0)
    multiply(4, 1)
    multiply(4, 2)
    core_copy(4).start()
    for i in (1, 2, 3):
        link(P2, 1, i).wait_recv()
        link(Q2, 1, i).start()
    y_finish(2)
    split_far(P2, 1)
    core_finish(4)
    for i in range(N_P2):
        link(Q2, 1, i).wait_recv()
    split_far(Q2, 1)
    multiply(5, 0)
    multiply(5, 1)
    core_copy(5).start()
    y_finish(3)
    for i in range(N_M2):
        link(M2, 1, i).wait_recv()
    for batch in range(4):
        deliver(batch)
    split_far(M2, 1)
    multiply(6, 0)
    multiply(6, 1)
    core_copy(6).start()
    core_finish(5)
    core_finish(6)
    for batch in (4, 5, 6):
        y_finish(batch)
        deliver(batch)

    for d in [0, 1, 2, 6, 7, 8, 3, 4, 5]:
        slots = [d, d + 6] if d in (3, 4, 5) else [d]
        for b in range(2):
            total = None
            for slot in slots:
                for src in range(2):
                    pltpu.make_async_copy(fin.at[slot, src, b], fin.at[slot, src, b],
                                          fin_recv.at[slot * 4 + src * 2 + b]).wait()
                term = fin[slot, 0, b] + fin[slot, 1, b]
                total = term if total is None else total + term
            out[d, :, b * 256:(b + 1) * 256] = total

    for half in range(2):
        for slot, n in ((P1, 4), (M1, 4), (Q1, 4), (M2, N_M2), (P2, N_P2), (Q2, N_P2)):
            for i in range(n):
                link(slot, half, i).wait_send()
    for batch in range(len(BATCHES)):
        deliver(batch, wait=True)


def per_device(factors):
    aux, orbitals, width = factors.shape
    chunk = aux // 8
    dma = pltpu.SemaphoreType.DMA
    n = len(BATCHES)
    out = pl.pallas_call(
        kernel,
        out_shape=jax.ShapeDtypeStruct((9, 32, width), jnp.float32),
        in_specs=[pl.BlockSpec(memory_space=pl.ANY)],
        out_specs=pl.BlockSpec(memory_space=pltpu.VMEM),
        scratch_shapes=[
            pltpu.VMEM((3, 2, aux, orbitals, 256), jnp.float32),
            pltpu.VMEM((2, N_M2, chunk, orbitals, 256), jnp.float32),
            pltpu.VMEM((2, N_P2, chunk, orbitals, 256), jnp.float32),
            pltpu.VMEM((2, N_P2, chunk, orbitals, 256), jnp.float32),
            pltpu.VMEM((aux, orbitals, 256), jnp.float32),
            pltpu.VMEM((6, 2, 8, chunk * orbitals, 256), jnp.bfloat16),
            pltpu.VMEM((6, 2, 8, chunk * orbitals, 256), jnp.bfloat16),
            pltpu.VMEM((2, TILES, 4, 32, 256), jnp.float32),
            pltpu.VMEM((TILES, 4, 32, 256), jnp.float32),
            pltpu.VMEM((3, TILES, 32, 256), jnp.float32),
            pltpu.VMEM((12, 2, 2, 32, 256), jnp.float32),
            dma((50,)), dma((50,)), dma, dma((n,)), dma((n,)), dma((3 * n,)), dma((3 * n,)), dma((TILES,)), dma((48,)),
        ],
        compiler_params=pltpu.CompilerParams(
            collective_id=0, has_side_effects=True, vmem_limit_bytes=62 * 2**20),
        cost_estimate=pl.CostEstimate(flops=6 * 9 * 512 * 512 * aux * orbitals, bytes_accessed=4 * 2**20,
                                      transcendentals=0),
        name="exchange",
    )(factors)
    return out[:, :, None, :]


def solution(mesh):
    return jax.shard_map(
        per_device,
        mesh=mesh,
        in_specs=(P("grp", None, "blk"),),
        out_specs=P(None, "grp", "blk", None),
        check_vma=False,
    )
```

```python
import jax
import jax.numpy as jnp
from jax import lax
from jax.experimental import pallas as pl
from jax.experimental.pallas import tpu as pltpu
from jax.sharding import PartitionSpec as P

MESH = pl.DeviceIdType.MESH
OWN, P1, M1, Q1, M2, P2, Q2 = range(7)
OFFSET = [(0, 0), (0, 1), (0, -1), (1, 1), (0, -2), (0, 2), (1, 2)]
ORDER = [0, 3, 5, 2, 7, 1, 4, 6]
N_M2, N_P2 = 5, 4


def pairs(s, t, halves):
    return [(s, i, t, j) for i, j in halves]


ALL = [(0, 0), (0, 1), (1, 0), (1, 1)]
A, B = [(0, 0), (0, 1)], [(1, 0), (1, 1)]
BATCHES = [
    [(8, pairs(OWN, OWN, ALL))],
    [(8, pairs(P1, OWN, A) + pairs(P1, M1, ALL[:1])), (8, pairs(Q1, OWN, A) + pairs(Q1, P1, ALL[:1]) + pairs(Q1, M1, ALL[:1]))],
    [(8, pairs(P1, OWN, B) + pairs(P1, M1, ALL[1:]) + pairs(Q1, P1, ALL[1:2]) + pairs(Q1, M1, ALL[1:2]))],
    [(8, pairs(Q1, OWN, B) + pairs(Q1, P1, B) + pairs(Q1, M1, B))],
    [(5, pairs(M2, P1, A) + pairs(M2, Q1, A)), (3, pairs(P2, M1, A)), (4, pairs(M2, P2, ALL[:1]))],
    [(3, pairs(Q2, M1, A)), (4, pairs(M2, Q2, ALL[:1]))],
    [(3, pairs(P2, M1, B)), (4, pairs(M2, P2, ALL[1:2]))],
    [(3, pairs(Q2, M1, B)), (4, pairs(M2, Q2, ALL[1:2]))],
    [(4, pairs(M2, P2, B) + pairs(M2, Q2, B))],
    [(5, pairs(M2, P1, B) + pairs(M2, Q1, B))],
]
FIRST, COUNT = [], []
for batch in BATCHES:
    FIRST.append(sum(COUNT))
    COUNT.append(sum(len(tiles) for _, tiles in batch))
TILES = sum(COUNT)


def pick(t, values):
    out = values[0]
    for k in range(1, len(values)):
        if values[k] != values[k - 1]:
            out = jnp.where(t >= k, values[k], out)
    return out


def kernel(x, out, near, m2, p2, q2, own, hi, lo, prod, core_in, y_in, fin,
           link_send, link_recv, own_sem, core_send, core_recv, y_send, y_recv, fin_send, fin_recv):
    grp, blk = lax.axis_index("grp"), lax.axis_index("blk")
    core, y, h = lax.rem(grp, 2), lax.rem(lax.div(grp, 2), 4), lax.div(grp, 8)
    z, row = lax.rem(blk, 8), lax.div(blk, 8)
    chunk = near.shape[2] // 8
    piece = near.shape[2] // 4

    def at_blk(dl, dz):
        return lax.rem(row + dl, 2) * 8 + lax.rem(z + dz + 8, 8)

    def at_grp(dh, dy, dk):
        return lax.rem(h + dh, 2) * 8 + lax.rem(y + dy, 4) * 2 + lax.rem(core + dk, 2)

    greet = [(grp, at_blk(1, 0)), (at_grp(0, 0, 1), blk)]
    greet += [(at_grp(0, dy, 0), blk) for dy in (1, 2, 3)]
    plane = [(0, 0), (0, 1), (0, -1), (0, 2), (0, -2), (1, 1), (1, -1), (1, 2), (1, -2)]
    for dh in range(2):
        greet += [(at_grp(dh, 0, 0), at_blk(dl, dz)) for dl, dz in plane if (dh, dl, dz) != (0, 0, 0)]
    barrier = pltpu.get_barrier_semaphore()
    for dev in greet:
        pl.semaphore_signal(barrier, inc=1, device_id=dev, device_id_type=MESH)
    pl.semaphore_wait(barrier, len(greet))

    down, up, across = (grp, at_blk(0, -1)), (grp, at_blk(0, 1)), (grp, at_blk(1, 0))

    def remote(src, dst, sem, dev):
        return pltpu.make_async_remote_copy(src_ref=src, dst_ref=dst, send_sem=link_send.at[sem],
                                            recv_sem=link_recv.at[sem], device_id=dev, device_id_type=MESH)

    def link(slot, half, i):
        if slot in (P1, M1, Q1):
            span = pl.ds(i * piece, piece)
            src = near.at[P1 - 1, half, span] if slot == Q1 else x.at[span, :, pl.ds(half * 256, 256)]
            return remote(src, near.at[slot - 1, half, span], (slot - 1) * 8 + half * 4 + i,
                          {P1: down, M1: up, Q1: across}[slot])
        if slot == Q2:
            return remote(p2.at[half, i], q2.at[half, i], 42 + half * N_P2 + i, across)
        their_z = z + 1 if slot == M2 else z + 7
        span = pl.ds(lax.rem(their_z + 8 - ORDER[i], 8) * chunk, chunk)
        if slot == M2:
            return remote(near.at[M1 - 1, half, span], m2.at[half, i], 24 + half * N_M2 + i, up)
        return remote(near.at[P1 - 1, half, span], p2.at[half, i], 34 + half * N_P2 + i, down)

    for half in range(2):
        for i in range(4):
            link(P1, half, i).start()
            link(M1, half, i).start()

    def split(a, slot, half, p):
        a = a.reshape(-1, 256)
        top = a.astype(jnp.bfloat16)
        hi[slot, half, p] = top
        lo[slot, half, p] = (a - top.astype(jnp.float32)).astype(jnp.bfloat16)

    def span_at(p):
        return pl.ds(lax.rem(z + 8 - pick(p, ORDER), 8) * chunk, chunk)

    def split_near(slot, half):
        @pl.loop(0, 8)
        def _(p):
            split(near[slot - 1, half, span_at(p)], slot, half, p)

    def split_far(slot, half, start=0, stop=None):
        src, n, keep, base = {M2: (m2, N_M2, M2, 0), P2: (p2, N_P2, P2, 0), Q2: (q2, N_P2, P2, N_P2)}[slot]

        @pl.loop(start, n if stop is None else stop)
        def _(p):
            split(src[half, p], keep, half, base + p)

    for half in range(2):
        copy = pltpu.make_async_copy(x.at[:, :, pl.ds(half * 256, 256)], own, own_sem)
        copy.start()
        copy.wait()

        @pl.loop(0, 8)
        def _(p):
            split(own[span_at(p)], OWN, half, p)

    def where_is(slot):
        return at_blk(pick(slot, [dl for dl, _ in OFFSET]), pick(slot, [dz for _, dz in OFFSET]))

    def tile_at(tiles, t):
        s, i, u, j = (pick(t, list(field)) for field in zip(*tiles))
        one, two = where_is(s), where_is(u)
        diff = lax.rem(one - two + 16, 16)
        straight = diff <= 8
        pick2 = lambda p, q: jnp.where(straight, p, q)
        return (pick2(s, u), pick2(i, j), pick2(u, s), pick2(j, i), pick2(two, one), pick2(diff, 16 - diff))

    def multiply(batch, group):
        chunks, tiles = BATCHES[batch][group]
        start = FIRST[batch] + sum(len(g) for _, g in BATCHES[batch][:group])

        @pl.loop(0, len(tiles))
        def _(t):
            rows, a, cols, b, _, _ = tile_at(tiles, t)

            def load(buf, slot, half):
                base = 0 if chunks == 8 else jnp.where(slot == Q2, N_P2, 0)
                kept = slot if chunks == 8 else jnp.where(slot == Q2, P2, slot)
                return buf[kept, half, pl.ds(base, chunks)].reshape(-1, 256)

            total = None
            for left, right in ((hi, hi), (hi, lo), (lo, hi)):
                term = lax.dot_general(load(left, rows, a), load(right, cols, b), (((0,), (0,)), ((), ())),
                                       preferred_element_type=jnp.float32)
                total = term if total is None else total + term
            total = total.reshape(4, 2, 32, 256)
            prod[0, start + t] = total[:, 0]
            prod[1, start + t] = total[:, 1]

    def core_copy(batch):
        span = pl.ds(FIRST[batch], COUNT[batch])
        return pltpu.make_async_remote_copy(
            src_ref=prod.at[1 - core, span], dst_ref=core_in.at[span],
            send_sem=core_send.at[batch], recv_sem=core_recv.at[batch],
            device_id=(at_grp(0, 0, 1), blk), device_id_type=MESH)

    def y_copy(batch, leg):
        first, count = FIRST[batch], COUNT[batch]
        first, count = [(first, count // 2), (first + count // 2, count - count // 2), (first, count), (first, count)][leg]
        strip, dy, land = [(2, 1, 0), (2, 3, 0), (1, 1, 1), (3, 3, 2)][leg]
        span = pl.ds(first, count)
        return pltpu.make_async_remote_copy(
            src_ref=prod.at[core, span, lax.rem(y + strip, 4)], dst_ref=y_in.at[land, span],
            send_sem=y_send.at[batch * 4 + leg], recv_sem=y_recv.at[batch * 4 + leg],
            device_id=(at_grp(0, dy, 0), blk), device_id_type=MESH)

    def y_begin(batch):
        y_copy(batch, 0).start()
        y_copy(batch, 1).start()

    def y_turn(batch):
        first, count = FIRST[batch], COUNT[batch]
        y_copy(batch, 0).wait()
        y_copy(batch, 1).wait()

        @pl.loop(first, first + count)
        def _(q):
            strip = jnp.where(q < first + count // 2, lax.rem(y + 1, 4), lax.rem(y + 3, 4))
            prod[core, q, strip] = prod[core, q, strip] + y_in[0, q]

        y_copy(batch, 2).start()
        y_copy(batch, 3).start()

    def core_finish(batch):
        core_copy(batch).wait()

        @pl.loop(FIRST[batch], FIRST[batch] + COUNT[batch])
        def _(q):
            prod[core, q] = prod[core, q] + core_in[q]

        y_begin(batch)

    def y_finish(batch):
        y_copy(batch, 2).wait()
        y_copy(batch, 3).wait()

        @pl.loop(FIRST[batch], FIRST[batch] + COUNT[batch])
        def _(q):
            prod[core, q, y] = prod[core, q, y] + (y_in[1, q] + y_in[2, q])

    def deliver(batch, wait=False):
        start = FIRST[batch]
        for chunks, tiles in BATCHES[batch]:
            @pl.loop(0, len(tiles))
            def _(t, chunks=chunks, tiles=tiles, start=start):
                _, a, _, b, owner, distance = tile_at(tiles, t)
                place = {8: 0, 5: 0, 3: 1, 4: lax.div(z, 4)}[chunks]
                slot = distance + 6 * place
                src, sem = prod.at[core, start + t, y], slot * 4 + h * 2 + b
                mine = jnp.logical_and(a == h, owner == blk)
                if not wait:
                    @pl.when(mine)
                    def _():
                        pltpu.make_async_copy(src, fin.at[slot, h, b], fin_recv.at[sem]).start()

                @pl.when(jnp.logical_not(mine))
                def _():
                    copy = pltpu.make_async_remote_copy(
                        src_ref=src, dst_ref=fin.at[slot, h, b], send_sem=fin_send.at[start + t],
                        recv_sem=fin_recv.at[sem], device_id=(a * 8 + y * 2 + core, owner), device_id_type=MESH)
                    if wait:
                        copy.wait_send()
                    else:
                        copy.start()
            start += len(tiles)

    def pass_on(slot, then, half, pieces):
        for i in pieces:
            link(slot, half, i).wait_recv()
            link(then, half, i).start()

    def arrive(slot, half, pieces):
        for i in pieces:
            link(slot, half, i).wait_recv()

    def second_hops(half):
        for i in range(N_M2):
            if i < N_P2:
                link(P2, half, i).start()
            link(M2, half, i).start()

    multiply(0, 0)
    core_copy(0).start()
    pass_on(P1, Q1, 0, [0])
    core_finish(0)
    pass_on(P1, Q1, 0, [1])
    y_turn(0)
    pass_on(P1, Q1, 0, [2, 3])
    arrive(M1, 0, range(4))
    second_hops(0)
    split_near(P1, 0)
    split_near(M1, 0)
    multiply(1, 0)
    y_finish(0)
    pass_on(P1, Q1, 1, [0])
    arrive(Q1, 0, range(4))
    split_near(Q1, 0)
    multiply(1, 1)
    core_copy(1).start()
    pass_on(P1, Q1, 1, [1])
    core_finish(1)
    pass_on(P1, Q1, 1, [2])
    y_turn(1)
    pass_on(P1, Q1, 1, [3])
    arrive(M1, 1, range(4))
    second_hops(1)
    split_near(P1, 1)
    split_near(M1, 1)
    multiply(2, 0)
    core_copy(2).start()
    y_finish(1)
    pass_on(P2, Q2, 0, [0, 1])
    core_finish(2)
    arrive(Q1, 1, range(4))
    split_near(Q1, 1)
    multiply(3, 0)
    core_copy(3).start()
    pass_on(P2, Q2, 0, [2, 3])
    y_turn(2)
    split_far(P2, 0)
    core_finish(3)
    arrive(M2, 0, range(N_M2))
    split_far(M2, 0)
    for group in range(3):
        multiply(4, group)
    core_copy(4).start()
    y_finish(2)
    y_turn(3)
    pass_on(P2, Q2, 1, [0])
    arrive(Q2, 0, range(N_P2))
    split_far(Q2, 0)
    for group in range(2):
        multiply(5, group)
    core_copy(5).start()
    core_finish(4)
    pass_on(P2, Q2, 1, [1])
    y_finish(3)
    core_finish(5)
    pass_on(P2, Q2, 1, [2])
    y_turn(4)
    pass_on(P2, Q2, 1, [3])
    split_far(P2, 1)
    for group in range(2):
        multiply(6, group)
    core_copy(6).start()
    y_turn(5)
    y_finish(4)
    core_finish(6)
    arrive(Q2, 1, range(N_P2))
    split_far(Q2, 1)
    for group in range(2):
        multiply(7, group)
    core_copy(7).start()
    y_finish(5)
    y_turn(6)
    arrive(M2, 1, range(N_P2))
    split_far(M2, 1, 0, N_P2)
    multiply(8, 0)
    core_copy(8).start()
    core_finish(7)
    deliver(0)
    deliver(1)
    arrive(M2, 1, range(N_P2, N_M2))
    split_far(M2, 1, N_P2)
    multiply(9, 0)
    core_copy(9).start()
    core_finish(8)
    deliver(2)
    deliver(3)
    y_turn(7)
    y_finish(6)
    deliver(4)
    core_finish(9)
    deliver(5)
    deliver(6)
    y_turn(8)
    y_finish(7)
    deliver(7)
    y_turn(9)
    y_finish(8)
    deliver(8)
    y_finish(9)
    deliver(9)

    for d in [0, 1, 2, 6, 7, 8, 3, 4, 5]:
        slots = [d, d + 6] if d in (3, 4, 5) else [d]
        for b in range(2):
            total = None
            for slot in slots:
                for src in range(2):
                    pltpu.make_async_copy(fin.at[slot, src, b], fin.at[slot, src, b],
                                          fin_recv.at[slot * 4 + src * 2 + b]).wait()
                term = fin[slot, 0, b] + fin[slot, 1, b]
                total = term if total is None else total + term
            out[d, :, b * 256:(b + 1) * 256] = total

    for half in range(2):
        for slot, n in ((P1, 4), (M1, 4), (Q1, 4), (M2, N_M2), (P2, N_P2), (Q2, N_P2)):
            for i in range(n):
                link(slot, half, i).wait_send()
    for batch in range(len(BATCHES)):
        deliver(batch, wait=True)


def per_device(factors):
    aux, orbitals, width = factors.shape
    chunk = aux // 8
    dma = pltpu.SemaphoreType.DMA
    n = len(BATCHES)
    out = pl.pallas_call(
        kernel,
        out_shape=jax.ShapeDtypeStruct((9, 32, width), jnp.float32),
        in_specs=[pl.BlockSpec(memory_space=pl.ANY)],
        out_specs=pl.BlockSpec(memory_space=pltpu.VMEM),
        scratch_shapes=[
            pltpu.VMEM((3, 2, aux, orbitals, 256), jnp.float32),
            pltpu.VMEM((2, N_M2, chunk, orbitals, 256), jnp.float32),
            pltpu.VMEM((2, N_P2, chunk, orbitals, 256), jnp.float32),
            pltpu.VMEM((2, N_P2, chunk, orbitals, 256), jnp.float32),
            pltpu.VMEM((aux, orbitals, 256), jnp.float32),
            pltpu.VMEM((6, 2, 8, chunk * orbitals, 256), jnp.bfloat16),
            pltpu.VMEM((6, 2, 8, chunk * orbitals, 256), jnp.bfloat16),
            pltpu.VMEM((2, TILES, 4, 32, 256), jnp.float32),
            pltpu.VMEM((TILES, 4, 32, 256), jnp.float32),
            pltpu.VMEM((3, TILES, 32, 256), jnp.float32),
            pltpu.VMEM((12, 2, 2, 32, 256), jnp.float32),
            dma((50,)), dma((50,)), dma, dma((n,)), dma((n,)), dma((4 * n,)), dma((4 * n,)), dma((TILES,)), dma((48,)),
        ],
        compiler_params=pltpu.CompilerParams(
            collective_id=0, has_side_effects=True, vmem_limit_bytes=62 * 2**20),
        cost_estimate=pl.CostEstimate(flops=6 * 9 * 512 * 512 * aux * orbitals, bytes_accessed=4 * 2**20,
                                      transcendentals=0),
        name="exchange",
    )(factors)
    return out[:, :, None, :]


def solution(mesh):
    return jax.shard_map(
        per_device,
        mesh=mesh,
        in_specs=(P("grp", None, "blk"),),
        out_specs=P(None, "grp", "blk", None),
        check_vma=False,
    )
```

```python
import jax
import jax.numpy as jnp
from jax import lax
from jax.experimental import pallas as pl
from jax.experimental.pallas import tpu as pltpu
from jax.sharding import PartitionSpec as P

MESH = pl.DeviceIdType.MESH
OWN, P1, M1, Q1, M2, P2, Q2 = range(7)
OFFSET = [(0, 0), (0, -1), (0, 1), (1, -1), (0, 2), (0, -2), (1, -2)]
ORDER = [0, 3, 5, 2, 7, 1, 4, 6]
N_M2, N_P2 = 5, 4
NEAR = 4


def pairs(s, t, halves):
    return [(s, i, t, j) for i, j in halves]


ALL = [(0, 0), (0, 1), (1, 0), (1, 1)]
A, B = [(0, 0), (0, 1)], [(1, 0), (1, 1)]
BATCHES = [
    [(8, pairs(OWN, OWN, ALL))],
    [(8, pairs(M1, OWN, A) + pairs(P1, M1, ALL[:1])), (8, pairs(Q1, OWN, A) + pairs(Q1, P1, ALL[:1]) + pairs(Q1, M1, ALL[:1]))],
    [(8, pairs(M1, OWN, B) + pairs(P1, M1, ALL[1:]) + pairs(Q1, P1, ALL[1:2]) + pairs(Q1, M1, ALL[1:2]))],
    [(8, pairs(Q1, OWN, B) + pairs(Q1, P1, B) + pairs(Q1, M1, B))],
    [(5, pairs(M2, P1, A) + pairs(M2, Q1, A)), (3, pairs(P2, M1, A)), (4, pairs(M2, P2, ALL[:1]))],
    [(3, pairs(Q2, M1, A)), (4, pairs(M2, Q2, ALL[:1]))],
    [(3, pairs(P2, M1, B)), (4, pairs(M2, P2, ALL[1:2]))],
    [(4, pairs(M2, P2, B) + pairs(M2, Q2, ALL[2:3]))],
    [(5, pairs(M2, P1, B) + pairs(M2, Q1, B))],
    [(3, pairs(Q2, M1, B)), (4, pairs(M2, Q2, [(0, 1), (1, 1)]))],
]
FIRST, COUNT = [], []
for batch in BATCHES:
    FIRST.append(sum(COUNT))
    COUNT.append(sum(len(tiles) for _, tiles in batch))
TILES = sum(COUNT)
DIRECT = ()


def pick(t, values):
    out = values[0]
    for k in range(1, len(values)):
        if values[k] != values[k - 1]:
            out = jnp.where(t >= k, values[k], out)
    return out


def kernel(x, out, near, m2, p2, q2, own, hi, lo, prod, core_in, y_in, fin,
           link_send, link_recv, own_sem, core_send, core_recv, y_send, y_recv, fin_send, fin_recv):
    grp, blk = lax.axis_index("grp"), lax.axis_index("blk")
    core, y, h = lax.rem(grp, 2), lax.rem(lax.div(grp, 2), 4), lax.div(grp, 8)
    z, row = lax.rem(blk, 8), lax.div(blk, 8)
    against = lax.rem(8 - z, 8)
    chunk = near.shape[2] // 8
    piece = near.shape[2] // NEAR

    def at_blk(dl, dz):
        return lax.rem(row + dl, 2) * 8 + lax.rem(z + dz + 8, 8)

    def at_grp(dh, dy, dk):
        return lax.rem(h + dh, 2) * 8 + lax.rem(y + dy, 4) * 2 + lax.rem(core + dk, 2)

    greet = [(grp, at_blk(1, 0)), (at_grp(0, 0, 1), blk)]
    greet += [(at_grp(0, dy, 0), blk) for dy in (1, 2, 3)]
    plane = [(0, 0), (0, 1), (0, -1), (0, 2), (0, -2), (1, 1), (1, -1), (1, 2), (1, -2)]
    for dh in range(2):
        greet += [(at_grp(dh, 0, 0), at_blk(dl, dz)) for dl, dz in plane if (dh, dl, dz) != (0, 0, 0)]
    barrier = pltpu.get_barrier_semaphore()
    for dev in greet:
        pl.semaphore_signal(barrier, inc=1, device_id=dev, device_id_type=MESH)
    pl.semaphore_wait(barrier, len(greet))

    ahead, back, across = (grp, at_blk(0, 1)), (grp, at_blk(0, -1)), (grp, at_blk(1, 0))

    def remote(src, dst, sem, dev):
        return pltpu.make_async_remote_copy(src_ref=src, dst_ref=dst, send_sem=link_send.at[sem],
                                            recv_sem=link_recv.at[sem], device_id=dev, device_id_type=MESH)

    def link(slot, half, i):
        if slot in (P1, M1, Q1):
            span = pl.ds(i * piece, piece)
            src = near.at[P1 - 1, half, span] if slot == Q1 else x.at[span, :, pl.ds(half * 256, 256)]
            return remote(src, near.at[slot - 1, half, span], ((slot - 1) * 2 + half) * NEAR + i,
                          {P1: ahead, M1: back, Q1: across}[slot])
        if slot == Q2:
            return remote(p2.at[half, i], q2.at[half, i], 6 * NEAR + 18 + half * N_P2 + i, across)
        theirs = against + (1 if slot == M2 else 7)
        span = pl.ds(lax.rem(theirs + 8 - ORDER[i], 8) * chunk, chunk)
        if slot == M2:
            return remote(near.at[M1 - 1, half, span], m2.at[half, i], 6 * NEAR + half * N_M2 + i, back)
        return remote(near.at[P1 - 1, half, span], p2.at[half, i], 6 * NEAR + 10 + half * N_P2 + i, ahead)

    for half in range(2):
        for i in range(NEAR):
            link(P1, half, i).start()
            link(M1, half, i).start()

    def split(a, slot, half, p):
        a = a.reshape(-1, 256)
        top = a.astype(jnp.bfloat16)
        hi[slot, half, p] = top
        lo[slot, half, p] = (a - top.astype(jnp.float32)).astype(jnp.bfloat16)

    def span_at(p):
        return pl.ds(lax.rem(against + 8 - pick(p, ORDER), 8) * chunk, chunk)

    def split_near(slot, half):
        @pl.loop(0, 8)
        def _(p):
            split(near[slot - 1, half, span_at(p)], slot, half, p)

    def split_far(slot, half, start=0, stop=None):
        src, n, keep, base = {M2: (m2, N_M2, M2, 0), P2: (p2, N_P2, P2, 0), Q2: (q2, N_P2, P2, N_P2)}[slot]

        @pl.loop(start, n if stop is None else stop)
        def _(p):
            split(src[half, p], keep, half, base + p)

    for half in range(2):
        copy = pltpu.make_async_copy(x.at[:, :, pl.ds(half * 256, 256)], own, own_sem)
        copy.start()
        copy.wait()

        @pl.loop(0, 8)
        def _(p):
            split(own[span_at(p)], OWN, half, p)

    def where_is(slot):
        return at_blk(pick(slot, [dl for dl, _ in OFFSET]), pick(slot, [dz for _, dz in OFFSET]))

    def tile_at(tiles, t):
        s, i, u, j = (pick(t, list(field)) for field in zip(*tiles))
        one, two = where_is(s), where_is(u)
        diff = lax.rem(one - two + 16, 16)
        straight = diff <= 8
        pick2 = lambda p, q: jnp.where(straight, p, q)
        return pick2(s, u), pick2(i, j), pick2(u, s), pick2(j, i)

    def multiply(batch, group, skip=0, take=None):
        chunks, tiles = BATCHES[batch][group]
        take = chunks if take is None else take
        start = FIRST[batch] + sum(len(g) for _, g in BATCHES[batch][:group])

        @pl.loop(0, len(tiles))
        def _(t):
            rows, a, cols, b = tile_at(tiles, t)

            def load(buf, slot, half):
                base = 0 if chunks == 8 else jnp.where(slot == Q2, N_P2, 0)
                kept = slot if chunks == 8 else jnp.where(slot == Q2, P2, slot)
                return buf[kept, half, pl.ds(base + skip, take)].reshape(-1, 256)

            total = None
            for left, right in ((hi, hi), (hi, lo), (lo, hi)):
                term = lax.dot_general(load(left, rows, a), load(right, cols, b), (((0,), (0,)), ((), ())),
                                       preferred_element_type=jnp.float32)
                total = term if total is None else total + term
            total = total.reshape(4, 2, 32, 256)
            for k in range(2):
                strips = total[:, k]
                prod[k, start + t] = prod[k, start + t] + strips if skip else strips

    def core_copy(batch):
        span = pl.ds(FIRST[batch], COUNT[batch])
        return pltpu.make_async_remote_copy(
            src_ref=prod.at[1 - core, span], dst_ref=core_in.at[span],
            send_sem=core_send.at[batch], recv_sem=core_recv.at[batch],
            device_id=(at_grp(0, 0, 1), blk), device_id_type=MESH)

    def y_copy(batch, leg):
        first, count = FIRST[batch], COUNT[batch]
        if batch in DIRECT:
            leg_strip, leg_land = leg + 1, leg
            span = pl.ds(first, count)
            return pltpu.make_async_remote_copy(
                src_ref=prod.at[core, span, lax.rem(y + leg_strip, 4)], dst_ref=y_in.at[leg_land, span],
                send_sem=y_send.at[batch * 4 + leg], recv_sem=y_recv.at[batch * 4 + leg],
                device_id=(at_grp(0, leg_strip, 0), blk), device_id_type=MESH)
        first, count = [(first, count // 2), (first + count // 2, count - count // 2), (first, count), (first, count)][leg]
        strip, dy, land = [(2, 1, 0), (2, 3, 0), (1, 1, 1), (3, 3, 2)][leg]
        span = pl.ds(first, count)
        return pltpu.make_async_remote_copy(
            src_ref=prod.at[core, span, lax.rem(y + strip, 4)], dst_ref=y_in.at[land, span],
            send_sem=y_send.at[batch * 4 + leg], recv_sem=y_recv.at[batch * 4 + leg],
            device_id=(at_grp(0, dy, 0), blk), device_id_type=MESH)

    def y_begin(batch):
        if batch in DIRECT:
            y_copy(batch, 2).start()
        y_copy(batch, 0).start()
        y_copy(batch, 1).start()

    def y_turn(batch):
        first, count = FIRST[batch], COUNT[batch]
        if batch in DIRECT:
            return
        y_copy(batch, 0).wait()
        y_copy(batch, 1).wait()

        @pl.loop(first, first + count)
        def _(q):
            strip = jnp.where(q < first + count // 2, lax.rem(y + 1, 4), lax.rem(y + 3, 4))
            prod[core, q, strip] = prod[core, q, strip] + y_in[0, q]

        y_copy(batch, 2).start()
        y_copy(batch, 3).start()

    def core_finish(batch):
        core_copy(batch).wait()

        @pl.loop(FIRST[batch], FIRST[batch] + COUNT[batch])
        def _(q):
            prod[core, q] = prod[core, q] + core_in[q]

        y_begin(batch)

    def y_finish(batch):
        for leg in (0, 1, 2) if batch in DIRECT else (2, 3):
            y_copy(batch, leg).wait()

        @pl.loop(FIRST[batch], FIRST[batch] + COUNT[batch])
        def _(q):
            total = prod[core, q, y] + (y_in[1, q] + y_in[2, q])
            prod[core, q, y] = total + y_in[0, q] if batch in DIRECT else total

    facts = {}
    for tiles_of in BATCHES:
        for chunks, tiles in tiles_of:
            for s, _, u, _ in tiles:
                if (s, u) not in facts:
                    one, two = at_blk(*OFFSET[s]), at_blk(*OFFSET[u])
                    diff = lax.rem(one - two + 16, 16)
                    straight = diff <= 8
                    place = {8: 0, 5: 0, 3: 1, 4: lax.div(z, 4)}[chunks]
                    facts[s, u] = (straight, jnp.where(straight, two, one), jnp.where(straight, diff, 16 - diff) + 6 * place)

    def deliver(batch, wait=False):
        start = FIRST[batch]
        for chunks, tiles in BATCHES[batch]:
            for pair in dict.fromkeys((s, u) for s, _, u, _ in tiles):
                halves = [(i, j) for s, i, u, j in tiles if (s, u) == pair]
                straight, owner, slot = facts[pair]

                @pl.loop(0, len(halves))
                def _(t, halves=halves, straight=straight, owner=owner, slot=slot, start=start):
                    i, j = (pick(t, list(side)) for side in zip(*halves))
                    a, b = jnp.where(straight, i, j), jnp.where(straight, j, i)
                    src, sem = prod.at[core, start + t, y], slot * 4 + h * 2 + b
                    mine = jnp.logical_and(a == h, owner == blk)
                    if not wait:
                        @pl.when(mine)
                        def _():
                            pltpu.make_async_copy(src, fin.at[slot, h, b], fin_recv.at[sem]).start()

                    @pl.when(jnp.logical_not(mine))
                    def _():
                        copy = pltpu.make_async_remote_copy(
                            src_ref=src, dst_ref=fin.at[slot, h, b], send_sem=fin_send.at[start + t],
                            recv_sem=fin_recv.at[sem], device_id=(a * 8 + y * 2 + core, owner), device_id_type=MESH)
                        if wait:
                            copy.wait_send()
                        else:
                            copy.start()
                start += len(halves)

    def pass_on(slot, then, half, pieces):
        for i in pieces:
            link(slot, half, i).wait_recv()
            link(then, half, i).start()

    def arrive(slot, half, pieces):
        for i in pieces:
            link(slot, half, i).wait_recv()

    def second_hops(half):
        for i in range(N_M2):
            if i < N_P2:
                link(P2, half, i).start()
            link(M2, half, i).start()

    multiply(0, 0)
    core_copy(0).start()
    pass_on(P1, Q1, 0, range(0, NEAR // 4))
    core_finish(0)
    pass_on(P1, Q1, 0, range(NEAR // 4, NEAR // 2))
    y_turn(0)
    pass_on(P1, Q1, 0, range(NEAR // 2, NEAR))
    arrive(M1, 0, range(NEAR))
    second_hops(0)
    split_near(P1, 0)
    split_near(M1, 0)
    multiply(1, 0)
    y_finish(0)
    deliver(0)
    pass_on(P1, Q1, 1, range(0, NEAR // 4))
    arrive(Q1, 0, range(NEAR))
    split_near(Q1, 0)
    multiply(1, 1)
    core_copy(1).start()
    pass_on(P1, Q1, 1, range(NEAR // 4, NEAR // 2))
    core_finish(1)
    pass_on(P1, Q1, 1, range(NEAR // 2, 3 * NEAR // 4))
    y_turn(1)
    pass_on(P1, Q1, 1, range(3 * NEAR // 4, NEAR))
    arrive(M1, 1, range(NEAR))
    second_hops(1)
    split_near(P1, 1)
    split_near(M1, 1)
    multiply(2, 0)
    core_copy(2).start()
    y_finish(1)
    deliver(1)
    pass_on(P2, Q2, 0, [0, 1])
    core_finish(2)
    arrive(Q1, 1, range(NEAR))
    split_near(Q1, 1)
    multiply(3, 0)
    core_copy(3).start()
    pass_on(P2, Q2, 0, [2, 3])
    y_turn(2)
    split_far(P2, 0)
    core_finish(3)
    arrive(M2, 0, range(N_M2))
    split_far(M2, 0)
    for group in range(3):
        multiply(4, group)
    core_copy(4).start()
    y_finish(2)
    y_turn(3)
    pass_on(P2, Q2, 1, [0])
    arrive(Q2, 0, range(N_P2))
    split_far(Q2, 0)
    for group in range(2):
        multiply(5, group)
    core_copy(5).start()
    core_finish(4)
    pass_on(P2, Q2, 1, [1])
    y_finish(3)
    core_finish(5)
    pass_on(P2, Q2, 1, [2])
    y_turn(4)
    y_turn(5)
    pass_on(P2, Q2, 1, [3])
    split_far(P2, 1)
    for group in range(2):
        multiply(6, group)
    core_copy(6).start()
    y_finish(4)
    arrive(M2, 1, range(N_P2))
    split_far(M2, 1, 0, N_P2)
    multiply(7, 0)
    core_copy(7).start()
    core_finish(6)
    multiply(8, 0, 0, N_P2)
    y_finish(5)
    core_finish(7)
    y_turn(6)
    deliver(2)
    deliver(3)
    arrive(M2, 1, range(N_P2, N_M2))
    split_far(M2, 1, N_P2)
    multiply(8, 0, N_P2, N_M2 - N_P2)
    core_copy(8).start()
    arrive(Q2, 1, range(N_P2))
    split_far(Q2, 1)
    for group in range(2):
        multiply(9, group)
    core_copy(9).start()
    deliver(4)
    y_turn(7)
    core_finish(8)
    deliver(5)
    core_finish(9)
    y_finish(6)
    deliver(6)
    y_turn(8)
    y_finish(7)
    deliver(7)
    y_turn(9)
    for half in range(2):
        for slot, n in ((P1, NEAR), (M1, NEAR), (Q1, NEAR), (M2, N_M2), (P2, N_P2), (Q2, N_P2)):
            for i in range(n):
                link(slot, half, i).wait_send()
    for batch in range(4):
        deliver(batch, wait=True)
    y_finish(8)
    deliver(8)
    for batch in range(4, 7):
        deliver(batch, wait=True)
    y_finish(9)
    deliver(9)

    for d in [0, 1, 2, 6, 7, 8, 3, 4, 5]:
        slots = [d, d + 6] if d in (3, 4, 5) else [d]
        for b in range(2):
            total = None
            for slot in slots:
                for src in range(2):
                    pltpu.make_async_copy(fin.at[slot, src, b], fin.at[slot, src, b],
                                          fin_recv.at[slot * 4 + src * 2 + b]).wait()
                term = fin[slot, 0, b] + fin[slot, 1, b]
                total = term if total is None else total + term
            out[d, :, b * 256:(b + 1) * 256] = total

    for batch in range(7, len(BATCHES)):
        deliver(batch, wait=True)


def per_device(factors):
    aux, orbitals, width = factors.shape
    chunk = aux // 8
    dma = pltpu.SemaphoreType.DMA
    n = len(BATCHES)
    out = pl.pallas_call(
        kernel,
        out_shape=jax.ShapeDtypeStruct((9, 32, width), jnp.float32),
        in_specs=[pl.BlockSpec(memory_space=pl.ANY)],
        out_specs=pl.BlockSpec(memory_space=pltpu.VMEM),
        scratch_shapes=[
            pltpu.VMEM((3, 2, aux, orbitals, 256), jnp.float32),
            pltpu.VMEM((2, N_M2, chunk, orbitals, 256), jnp.float32),
            pltpu.VMEM((2, N_P2, chunk, orbitals, 256), jnp.float32),
            pltpu.VMEM((2, N_P2, chunk, orbitals, 256), jnp.float32),
            pltpu.VMEM((aux, orbitals, 256), jnp.float32),
            pltpu.VMEM((6, 2, 8, chunk * orbitals, 256), jnp.bfloat16),
            pltpu.VMEM((6, 2, 8, chunk * orbitals, 256), jnp.bfloat16),
            pltpu.VMEM((2, TILES, 4, 32, 256), jnp.float32),
            pltpu.VMEM((TILES, 4, 32, 256), jnp.float32),
            pltpu.VMEM((3, TILES, 32, 256), jnp.float32),
            pltpu.VMEM((12, 2, 2, 32, 256), jnp.float32),
            dma((6 * NEAR + 26,)), dma((6 * NEAR + 26,)), dma, dma((n,)), dma((n,)), dma((4 * n,)), dma((4 * n,)), dma((TILES,)), dma((48,)),
        ],
        compiler_params=pltpu.CompilerParams(
            collective_id=0, has_side_effects=True, vmem_limit_bytes=62 * 2**20),
        cost_estimate=pl.CostEstimate(flops=6 * 9 * 512 * 512 * aux * orbitals, bytes_accessed=4 * 2**20,
                                      transcendentals=0),
        name="exchange",
    )(factors)
    return out[:, :, None, :]


def solution(mesh):
    return jax.shard_map(
        per_device,
        mesh=mesh,
        in_specs=(P("grp", None, "blk"),),
        out_specs=P(None, "grp", "blk", None),
        check_vma=False,
    )
```

```python
import jax
import jax.numpy as jnp
from jax import lax
from jax.experimental import pallas as pl
from jax.experimental.pallas import tpu as pltpu
from jax.sharding import PartitionSpec as P

MESH = pl.DeviceIdType.MESH
OWN, P1, M1, Q1, M2, P2, Q2 = range(7)
OFFSET = [(0, 0), (0, -1), (0, 1), (1, -1), (0, 2), (0, -2), (1, -2)]
ORDER = [0, 3, 5, 2, 7, 1, 4, 6]
N_M2, N_P2 = 5, 4
NEAR = 4


def pairs(s, t, halves):
    return [(s, i, t, j) for i, j in halves]


ALL = [(0, 0), (0, 1), (1, 0), (1, 1)]
A, B = [(0, 0), (0, 1)], [(1, 0), (1, 1)]
BATCHES = [
    [(8, pairs(OWN, OWN, ALL))],
    [(8, pairs(M1, OWN, A) + pairs(P1, M1, ALL[:1])), (8, pairs(Q1, OWN, A) + pairs(Q1, P1, ALL[:1]) + pairs(Q1, M1, ALL[:1]))],
    [(8, pairs(M1, OWN, B) + pairs(P1, M1, ALL[1:]) + pairs(Q1, P1, ALL[1:2]) + pairs(Q1, M1, ALL[1:2]))],
    [(8, pairs(Q1, OWN, B) + pairs(Q1, P1, B) + pairs(Q1, M1, B))],
    [(5, pairs(M2, P1, A) + pairs(M2, Q1, A)), (3, pairs(P2, M1, A)), (4, pairs(M2, P2, ALL[:1]))],
    [(3, pairs(Q2, M1, A)), (4, pairs(M2, Q2, ALL[:1]))],
    [(3, pairs(P2, M1, B)), (4, pairs(M2, P2, ALL[1:2]))],
    [(4, pairs(M2, P2, B) + pairs(M2, Q2, ALL[2:3]))],
    [(5, pairs(M2, P1, B) + pairs(M2, Q1, B))],
    [(3, pairs(Q2, M1, B)), (4, pairs(M2, Q2, [(0, 1), (1, 1)]))],
]
FIRST, COUNT = [], []
for batch in BATCHES:
    FIRST.append(sum(COUNT))
    COUNT.append(sum(len(tiles) for _, tiles in batch))
TILES = sum(COUNT)
DIRECT = ()


def pick(t, values):
    out = values[0]
    for k in range(1, len(values)):
        if values[k] != values[k - 1]:
            out = jnp.where(t >= k, values[k], out)
    return out


def kernel(x, out, near, m2, p2, q2, own, hi, lo, prod, core_in, y_in, fin,
           link_send, link_recv, own_sem, core_send, core_recv, y_send, y_recv, fin_send, fin_recv):
    grp, blk = lax.axis_index("grp"), lax.axis_index("blk")
    core, y, h = lax.rem(grp, 2), lax.rem(lax.div(grp, 2), 4), lax.div(grp, 8)
    z, row = lax.rem(blk, 8), lax.div(blk, 8)
    against = lax.rem(8 - z, 8)
    chunk = near.shape[2] // 8
    piece = near.shape[2] // NEAR

    def at_blk(dl, dz):
        return lax.rem(row + dl, 2) * 8 + lax.rem(z + dz + 8, 8)

    def at_grp(dh, dy, dk):
        return lax.rem(h + dh, 2) * 8 + lax.rem(y + dy, 4) * 2 + lax.rem(core + dk, 2)

    greet = [(grp, at_blk(1, 0)), (at_grp(0, 0, 1), blk)]
    greet += [(at_grp(0, dy, 0), blk) for dy in (1, 2, 3)]
    plane = [(0, 0), (0, 1), (0, -1), (0, 2), (0, -2), (1, 1), (1, -1), (1, 2), (1, -2)]
    for dh in range(2):
        greet += [(at_grp(dh, 0, 0), at_blk(dl, dz)) for dl, dz in plane if (dh, dl, dz) != (0, 0, 0)]
    barrier = pltpu.get_barrier_semaphore()
    for dev in greet:
        pl.semaphore_signal(barrier, inc=1, device_id=dev, device_id_type=MESH)
    pl.semaphore_wait(barrier, len(greet))

    ahead, back, across = (grp, at_blk(0, 1)), (grp, at_blk(0, -1)), (grp, at_blk(1, 0))

    def remote(src, dst, sem, dev):
        return pltpu.make_async_remote_copy(src_ref=src, dst_ref=dst, send_sem=link_send.at[sem],
                                            recv_sem=link_recv.at[sem], device_id=dev, device_id_type=MESH)

    def link(slot, half, i):
        if slot in (P1, M1, Q1):
            span = pl.ds(i * piece, piece)
            src = near.at[P1 - 1, half, span] if slot == Q1 else x.at[span, :, pl.ds(half * 256, 256)]
            return remote(src, near.at[slot - 1, half, span], ((slot - 1) * 2 + half) * NEAR + i,
                          {P1: ahead, M1: back, Q1: across}[slot])
        if slot == Q2:
            return remote(p2.at[half, i], q2.at[half, i], 6 * NEAR + 18 + half * N_P2 + i, across)
        theirs = against + (1 if slot == M2 else 7)
        span = pl.ds(lax.rem(theirs + 8 - ORDER[i], 8) * chunk, chunk)
        if slot == M2:
            return remote(near.at[M1 - 1, half, span], m2.at[half, i], 6 * NEAR + half * N_M2 + i, back)
        return remote(near.at[P1 - 1, half, span], p2.at[half, i], 6 * NEAR + 10 + half * N_P2 + i, ahead)

    for half in range(2):
        for i in range(NEAR):
            link(P1, half, i).start()
            link(M1, half, i).start()

    def split(a, slot, half, p):
        a = a.reshape(-1, 256)
        top = a.astype(jnp.bfloat16)
        hi[slot, half, p] = top
        lo[slot, half, p] = (a - top.astype(jnp.float32)).astype(jnp.bfloat16)

    def span_at(p):
        return pl.ds(lax.rem(against + 8 - pick(p, ORDER), 8) * chunk, chunk)

    def split_near(slot, half):
        @pl.loop(0, 8)
        def _(p):
            split(near[slot - 1, half, span_at(p)], slot, half, p)

    def split_far(slot, half, start=0, stop=None):
        src, n, keep, base = {M2: (m2, N_M2, M2, 0), P2: (p2, N_P2, P2, 0), Q2: (q2, N_P2, P2, N_P2)}[slot]

        @pl.loop(start, n if stop is None else stop)
        def _(p):
            split(src[half, p], keep, half, base + p)

    for half in range(2):
        copy = pltpu.make_async_copy(x.at[:, :, pl.ds(half * 256, 256)], own, own_sem)
        copy.start()
        copy.wait()

        @pl.loop(0, 8)
        def _(p):
            split(own[span_at(p)], OWN, half, p)

    def where_is(slot):
        return at_blk(pick(slot, [dl for dl, _ in OFFSET]), pick(slot, [dz for _, dz in OFFSET]))

    def tile_at(tiles, t):
        s, i, u, j = (pick(t, list(field)) for field in zip(*tiles))
        one, two = where_is(s), where_is(u)
        diff = lax.rem(one - two + 16, 16)
        straight = diff <= 8
        pick2 = lambda p, q: jnp.where(straight, p, q)
        return pick2(s, u), pick2(i, j), pick2(u, s), pick2(j, i)

    def multiply(batch, group, skip=0, take=None):
        chunks, tiles = BATCHES[batch][group]
        take = chunks if take is None else take
        start = FIRST[batch] + sum(len(g) for _, g in BATCHES[batch][:group])

        @pl.loop(0, len(tiles))
        def _(t):
            rows, a, cols, b = tile_at(tiles, t)

            def load(buf, slot, half):
                base = 0 if chunks == 8 else jnp.where(slot == Q2, N_P2, 0)
                kept = slot if chunks == 8 else jnp.where(slot == Q2, P2, slot)
                return buf[kept, half, pl.ds(base + skip, take)].reshape(-1, 256)

            total = None
            for left, right in ((hi, hi), (hi, lo), (lo, hi)):
                term = lax.dot_general(load(left, rows, a), load(right, cols, b), (((0,), (0,)), ((), ())),
                                       preferred_element_type=jnp.float32)
                total = term if total is None else total + term
            total = total.reshape(4, 2, 32, 256)
            for k in range(2):
                strips = total[:, k]
                prod[k, start + t] = prod[k, start + t] + strips if skip else strips

    def core_copy(batch):
        span = pl.ds(FIRST[batch], COUNT[batch])
        return pltpu.make_async_remote_copy(
            src_ref=prod.at[1 - core, span], dst_ref=core_in.at[span],
            send_sem=core_send.at[batch], recv_sem=core_recv.at[batch],
            device_id=(at_grp(0, 0, 1), blk), device_id_type=MESH)

    def y_copy(batch, leg):
        first, count = FIRST[batch], COUNT[batch]
        if batch in DIRECT:
            leg_strip, leg_land = leg + 1, leg
            span = pl.ds(first, count)
            return pltpu.make_async_remote_copy(
                src_ref=prod.at[core, span, lax.rem(y + leg_strip, 4)], dst_ref=y_in.at[leg_land, span],
                send_sem=y_send.at[batch * 4 + leg], recv_sem=y_recv.at[batch * 4 + leg],
                device_id=(at_grp(0, leg_strip, 0), blk), device_id_type=MESH)
        first, count = [(first, count // 2), (first + count // 2, count - count // 2), (first, count), (first, count)][leg]
        strip, dy, land = [(2, 1, 0), (2, 3, 0), (1, 1, 1), (3, 3, 2)][leg]
        span = pl.ds(first, count)
        return pltpu.make_async_remote_copy(
            src_ref=prod.at[core, span, lax.rem(y + strip, 4)], dst_ref=y_in.at[land, span],
            send_sem=y_send.at[batch * 4 + leg], recv_sem=y_recv.at[batch * 4 + leg],
            device_id=(at_grp(0, dy, 0), blk), device_id_type=MESH)

    def y_begin(batch):
        if batch in DIRECT:
            y_copy(batch, 2).start()
        y_copy(batch, 0).start()
        y_copy(batch, 1).start()

    def y_turn(batch):
        first, count = FIRST[batch], COUNT[batch]
        if batch in DIRECT:
            return
        y_copy(batch, 0).wait()
        y_copy(batch, 1).wait()

        @pl.loop(first, first + count)
        def _(q):
            strip = jnp.where(q < first + count // 2, lax.rem(y + 1, 4), lax.rem(y + 3, 4))
            prod[core, q, strip] = prod[core, q, strip] + y_in[0, q]

        y_copy(batch, 2).start()
        y_copy(batch, 3).start()

    def core_finish(batch):
        core_copy(batch).wait()

        @pl.loop(FIRST[batch], FIRST[batch] + COUNT[batch])
        def _(q):
            prod[core, q] = prod[core, q] + core_in[q]

        y_begin(batch)

    def y_finish(batch):
        for leg in (0, 1, 2) if batch in DIRECT else (2, 3):
            y_copy(batch, leg).wait()

        @pl.loop(FIRST[batch], FIRST[batch] + COUNT[batch])
        def _(q):
            total = prod[core, q, y] + (y_in[1, q] + y_in[2, q])
            prod[core, q, y] = total + y_in[0, q] if batch in DIRECT else total

    facts = {}
    for tiles_of in BATCHES:
        for chunks, tiles in tiles_of:
            for s, _, u, _ in tiles:
                if (s, u) not in facts:
                    one, two = at_blk(*OFFSET[s]), at_blk(*OFFSET[u])
                    diff = lax.rem(one - two + 16, 16)
                    straight = diff <= 8
                    place = {8: 0, 5: 0, 3: 1, 4: lax.div(z, 4)}[chunks]
                    facts[s, u] = (straight, jnp.where(straight, two, one), jnp.where(straight, diff, 16 - diff) + 6 * place)

    def deliver(batch, wait=False):
        start = FIRST[batch]
        for chunks, tiles in BATCHES[batch]:
            for pair in dict.fromkeys((s, u) for s, _, u, _ in tiles):
                halves = [(i, j) for s, i, u, j in tiles if (s, u) == pair]
                straight, owner, slot = facts[pair]

                @pl.loop(0, len(halves))
                def _(t, halves=halves, straight=straight, owner=owner, slot=slot, start=start):
                    i, j = (pick(t, list(side)) for side in zip(*halves))
                    a, b = jnp.where(straight, i, j), jnp.where(straight, j, i)
                    src, sem = prod.at[core, start + t, y], slot * 4 + h * 2 + b
                    mine = jnp.logical_and(a == h, owner == blk)
                    if not wait:
                        @pl.when(mine)
                        def _():
                            pltpu.make_async_copy(src, fin.at[slot, h, b], fin_recv.at[sem]).start()

                    @pl.when(jnp.logical_not(mine))
                    def _():
                        copy = pltpu.make_async_remote_copy(
                            src_ref=src, dst_ref=fin.at[slot, h, b], send_sem=fin_send.at[start + t],
                            recv_sem=fin_recv.at[sem], device_id=(a * 8 + y * 2 + core, owner), device_id_type=MESH)
                        if wait:
                            copy.wait_send()
                        else:
                            copy.start()
                start += len(halves)

    def collect(distances):
        for d in distances:
            slots = [d, d + 6] if d in (3, 4, 5) else [d]
            for b in range(2):
                total = None
                for slot in slots:
                    for src in range(2):
                        pltpu.make_async_copy(fin.at[slot, src, b], fin.at[slot, src, b],
                                              fin_recv.at[slot * 4 + src * 2 + b]).wait()
                    term = fin[slot, 0, b] + fin[slot, 1, b]
                    total = term if total is None else total + term
                out[d, :, b * 256:(b + 1) * 256] = total

    def pass_on(slot, then, half, pieces):
        for i in pieces:
            link(slot, half, i).wait_recv()
            link(then, half, i).start()

    def arrive(slot, half, pieces):
        for i in pieces:
            link(slot, half, i).wait_recv()

    def second_hops(half):
        for i in range(N_M2):
            if i < N_P2:
                link(P2, half, i).start()
            link(M2, half, i).start()

    multiply(0, 0)
    core_copy(0).start()
    pass_on(P1, Q1, 0, range(0, NEAR // 4))
    core_finish(0)
    pass_on(P1, Q1, 0, range(NEAR // 4, NEAR // 2))
    y_turn(0)
    pass_on(P1, Q1, 0, range(NEAR // 2, NEAR))
    arrive(M1, 0, range(NEAR))
    second_hops(0)
    split_near(P1, 0)
    split_near(M1, 0)
    multiply(1, 0)
    y_finish(0)
    deliver(0)
    pass_on(P1, Q1, 1, range(0, NEAR // 4))
    arrive(Q1, 0, range(NEAR))
    split_near(Q1, 0)
    multiply(1, 1)
    core_copy(1).start()
    pass_on(P1, Q1, 1, range(NEAR // 4, NEAR // 2))
    core_finish(1)
    pass_on(P1, Q1, 1, range(NEAR // 2, 3 * NEAR // 4))
    y_turn(1)
    pass_on(P1, Q1, 1, range(3 * NEAR // 4, NEAR))
    arrive(M1, 1, range(NEAR))
    second_hops(1)
    split_near(P1, 1)
    split_near(M1, 1)
    multiply(2, 0)
    core_copy(2).start()
    y_finish(1)
    deliver(1)
    pass_on(P2, Q2, 0, [0, 1])
    core_finish(2)
    arrive(Q1, 1, range(NEAR))
    split_near(Q1, 1)
    multiply(3, 0)
    core_copy(3).start()
    pass_on(P2, Q2, 0, [2, 3])
    y_turn(2)
    split_far(P2, 0)
    core_finish(3)
    arrive(M2, 0, range(N_M2))
    split_far(M2, 0)
    for group in range(3):
        multiply(4, group)
    core_copy(4).start()
    y_finish(2)
    y_turn(3)
    pass_on(P2, Q2, 1, [0])
    arrive(Q2, 0, range(N_P2))
    split_far(Q2, 0)
    for group in range(2):
        multiply(5, group)
    core_copy(5).start()
    core_finish(4)
    pass_on(P2, Q2, 1, [1])
    y_finish(3)
    core_finish(5)
    pass_on(P2, Q2, 1, [2])
    y_turn(4)
    y_turn(5)
    pass_on(P2, Q2, 1, [3])
    split_far(P2, 1)
    for group in range(2):
        multiply(6, group)
    core_copy(6).start()
    y_finish(4)
    arrive(M2, 1, range(N_P2))
    split_far(M2, 1, 0, N_P2)
    multiply(7, 0)
    core_copy(7).start()
    core_finish(6)
    multiply(8, 0, 0, N_P2)
    y_finish(5)
    core_finish(7)
    y_turn(6)
    deliver(2)
    deliver(3)
    arrive(M2, 1, range(N_P2, N_M2))
    split_far(M2, 1, N_P2)
    multiply(8, 0, N_P2, N_M2 - N_P2)
    core_copy(8).start()
    arrive(Q2, 1, range(N_P2))
    split_far(Q2, 1)
    for group in range(2):
        multiply(9, group)
    core_copy(9).start()
    deliver(4)
    y_turn(7)
    core_finish(8)
    deliver(5)
    core_finish(9)
    y_finish(6)
    deliver(6)
    y_turn(8)
    y_finish(7)
    deliver(7)
    y_turn(9)
    for half in range(2):
        for slot, n in ((P1, NEAR), (M1, NEAR), (Q1, NEAR), (M2, N_M2), (P2, N_P2), (Q2, N_P2)):
            for i in range(n):
                link(slot, half, i).wait_send()
    for batch in range(4):
        deliver(batch, wait=True)
    y_finish(8)
    deliver(8)
    collect([0, 1, 2, 6, 7, 8])
    for batch in range(4, 7):
        deliver(batch, wait=True)
    y_finish(9)
    deliver(9)
    for batch in range(7, len(BATCHES)):
        deliver(batch, wait=True)
    collect([3, 4, 5])


def per_device(factors):
    aux, orbitals, width = factors.shape
    chunk = aux // 8
    dma = pltpu.SemaphoreType.DMA
    n = len(BATCHES)
    out = pl.pallas_call(
        kernel,
        out_shape=jax.ShapeDtypeStruct((9, 32, width), jnp.float32),
        in_specs=[pl.BlockSpec(memory_space=pl.ANY)],
        out_specs=pl.BlockSpec(memory_space=pltpu.VMEM),
        scratch_shapes=[
            pltpu.VMEM((3, 2, aux, orbitals, 256), jnp.float32),
            pltpu.VMEM((2, N_M2, chunk, orbitals, 256), jnp.float32),
            pltpu.VMEM((2, N_P2, chunk, orbitals, 256), jnp.float32),
            pltpu.VMEM((2, N_P2, chunk, orbitals, 256), jnp.float32),
            pltpu.VMEM((aux, orbitals, 256), jnp.float32),
            pltpu.VMEM((6, 2, 8, chunk * orbitals, 256), jnp.bfloat16),
            pltpu.VMEM((6, 2, 8, chunk * orbitals, 256), jnp.bfloat16),
            pltpu.VMEM((2, TILES, 4, 32, 256), jnp.float32),
            pltpu.VMEM((TILES, 4, 32, 256), jnp.float32),
            pltpu.VMEM((3, TILES, 32, 256), jnp.float32),
            pltpu.VMEM((12, 2, 2, 32, 256), jnp.float32),
            dma((6 * NEAR + 26,)), dma((6 * NEAR + 26,)), dma, dma((n,)), dma((n,)), dma((4 * n,)), dma((4 * n,)), dma((TILES,)), dma((48,)),
        ],
        compiler_params=pltpu.CompilerParams(
            collective_id=0, has_side_effects=True, vmem_limit_bytes=62 * 2**20),
        cost_estimate=pl.CostEstimate(flops=6 * 9 * 512 * 512 * aux * orbitals, bytes_accessed=4 * 2**20,
                                      transcendentals=0),
        name="exchange",
    )(factors)
    return out[:, :, None, :]


def solution(mesh):
    return jax.shard_map(
        per_device,
        mesh=mesh,
        in_specs=(P("grp", None, "blk"),),
        out_specs=P(None, "grp", "blk", None),
        check_vma=False,
    )
```

```python
import jax
import jax.numpy as jnp
from jax import lax
from jax.experimental import pallas as pl
from jax.experimental.pallas import tpu as pltpu
from jax.sharding import PartitionSpec as P

MESH = pl.DeviceIdType.MESH
OWN, P1, M1, Q1, M2, P2, Q2 = range(7)
OFFSET = [(0, 0), (0, -1), (0, 1), (1, -1), (0, 2), (0, -2), (1, -2)]
ORDER = [0, 3, 5, 2, 7, 1, 4, 6]
N_M2, N_P2 = 5, 4
NEAR = 4


def pairs(s, t, halves):
    return [(s, i, t, j) for i, j in halves]


ALL = [(0, 0), (0, 1), (1, 0), (1, 1)]
A, B = [(0, 0), (0, 1)], [(1, 0), (1, 1)]
BATCHES = [
    [(8, pairs(OWN, OWN, ALL))],
    [(8, pairs(M1, OWN, A) + pairs(P1, M1, ALL[:1])), (8, pairs(Q1, OWN, A) + pairs(Q1, P1, ALL[:1]) + pairs(Q1, M1, ALL[:1]))],
    [(8, pairs(M1, OWN, B) + pairs(P1, M1, ALL[1:]) + pairs(Q1, P1, ALL[1:2]) + pairs(Q1, M1, ALL[1:2]))],
    [(8, pairs(Q1, OWN, B) + pairs(Q1, P1, B) + pairs(Q1, M1, B))],
    [(5, pairs(M2, P1, A) + pairs(M2, Q1, A)), (3, pairs(P2, M1, A)), (4, pairs(M2, P2, ALL[:1]))],
    [(3, pairs(Q2, M1, A)), (4, pairs(M2, Q2, ALL[:1]))],
    [(3, pairs(P2, M1, B)), (4, pairs(M2, P2, ALL[1:2]))],
    [(4, pairs(M2, P2, B) + pairs(M2, Q2, ALL[2:3]))],
    [(5, pairs(M2, P1, B) + pairs(M2, Q1, B))],
    [(3, pairs(Q2, M1, B)), (4, pairs(M2, Q2, [(0, 1), (1, 1)]))],
]
FIRST, COUNT = [], []
for batch in BATCHES:
    FIRST.append(sum(COUNT))
    COUNT.append(sum(len(tiles) for _, tiles in batch))
TILES = sum(COUNT)
DIRECT = ()


def pick(t, values):
    out = values[0]
    for k in range(1, len(values)):
        if values[k] != values[k - 1]:
            out = jnp.where(t >= k, values[k], out)
    return out


def kernel(x, out, near, m2, p2, q2, own, hi, lo, prod, core_in, y_in, fin,
           link_send, link_recv, own_sem, core_send, core_recv, y_send, y_recv, fin_send, fin_recv):
    grp, blk = lax.axis_index("grp"), lax.axis_index("blk")
    core, y, h = lax.rem(grp, 2), lax.rem(lax.div(grp, 2), 4), lax.div(grp, 8)
    z, row = lax.rem(blk, 8), lax.div(blk, 8)
    against = lax.rem(8 - z, 8)
    chunk = near.shape[2] // 8
    piece = near.shape[2] // NEAR

    def at_blk(dl, dz):
        return lax.rem(row + dl, 2) * 8 + lax.rem(z + dz + 8, 8)

    def at_grp(dh, dy, dk):
        return lax.rem(h + dh, 2) * 8 + lax.rem(y + dy, 4) * 2 + lax.rem(core + dk, 2)

    greet = [(grp, at_blk(1, 0)), (at_grp(0, 0, 1), blk)]
    greet += [(at_grp(0, dy, 0), blk) for dy in (1, 2, 3)]
    plane = [(0, 0), (0, 1), (0, -1), (0, 2), (0, -2), (1, 1), (1, -1), (1, 2), (1, -2)]
    for dh in range(2):
        greet += [(at_grp(dh, 0, 0), at_blk(dl, dz)) for dl, dz in plane if (dh, dl, dz) != (0, 0, 0)]
    barrier = pltpu.get_barrier_semaphore()
    for dev in reversed(greet):
        pl.semaphore_signal(barrier, inc=1, device_id=dev, device_id_type=MESH)
    pl.semaphore_wait(barrier, len(greet))

    ahead, back, across = (grp, at_blk(0, 1)), (grp, at_blk(0, -1)), (grp, at_blk(1, 0))

    def remote(src, dst, sem, dev):
        return pltpu.make_async_remote_copy(src_ref=src, dst_ref=dst, send_sem=link_send.at[sem],
                                            recv_sem=link_recv.at[sem], device_id=dev, device_id_type=MESH)

    def link(slot, half, i):
        if slot in (P1, M1, Q1):
            span = pl.ds(i * piece, piece)
            src = near.at[P1 - 1, half, span] if slot == Q1 else x.at[span, :, pl.ds(half * 256, 256)]
            return remote(src, near.at[slot - 1, half, span], ((slot - 1) * 2 + half) * NEAR + i,
                          {P1: ahead, M1: back, Q1: across}[slot])
        if slot == Q2:
            return remote(p2.at[half, i], q2.at[half, i], 6 * NEAR + 18 + half * N_P2 + i, across)
        theirs = against + (1 if slot == M2 else 7)
        span = pl.ds(lax.rem(theirs + 8 - ORDER[i], 8) * chunk, chunk)
        if slot == M2:
            return remote(near.at[M1 - 1, half, span], m2.at[half, i], 6 * NEAR + half * N_M2 + i, back)
        return remote(near.at[P1 - 1, half, span], p2.at[half, i], 6 * NEAR + 10 + half * N_P2 + i, ahead)

    for half in range(2):
        for i in range(NEAR):
            link(P1, half, i).start()
            link(M1, half, i).start()

    def split(a, slot, half, p):
        a = a.reshape(-1, 256)
        top = a.astype(jnp.bfloat16)
        hi[slot, half, p] = top
        lo[slot, half, p] = (a - top.astype(jnp.float32)).astype(jnp.bfloat16)

    def span_at(p):
        return pl.ds(lax.rem(against + 8 - pick(p, ORDER), 8) * chunk, chunk)

    def split_near(slot, half):
        @pl.loop(0, 8)
        def _(p):
            split(near[slot - 1, half, span_at(p)], slot, half, p)

    def split_far(slot, half, start=0, stop=None):
        src, n, keep, base = {M2: (m2, N_M2, M2, 0), P2: (p2, N_P2, P2, 0), Q2: (q2, N_P2, P2, N_P2)}[slot]

        @pl.loop(start, n if stop is None else stop)
        def _(p):
            split(src[half, p], keep, half, base + p)

    for half in range(2):
        copy = pltpu.make_async_copy(x.at[:, :, pl.ds(half * 256, 256)], own, own_sem)
        copy.start()
        copy.wait()

        @pl.loop(0, 8)
        def _(p):
            split(own[span_at(p)], OWN, half, p)

    def where_is(slot):
        return at_blk(pick(slot, [dl for dl, _ in OFFSET]), pick(slot, [dz for _, dz in OFFSET]))

    def tile_at(tiles, t):
        s, i, u, j = (pick(t, list(field)) for field in zip(*tiles))
        one, two = where_is(s), where_is(u)
        diff = lax.rem(one - two + 16, 16)
        straight = diff <= 8
        pick2 = lambda p, q: jnp.where(straight, p, q)
        return pick2(s, u), pick2(i, j), pick2(u, s), pick2(j, i)

    def multiply(batch, group, skip=0, take=None):
        chunks, tiles = BATCHES[batch][group]
        take = chunks if take is None else take
        start = FIRST[batch] + sum(len(g) for _, g in BATCHES[batch][:group])

        @pl.loop(0, len(tiles))
        def _(t):
            rows, a, cols, b = tile_at(tiles, t)

            def load(buf, slot, half):
                base = 0 if chunks == 8 else jnp.where(slot == Q2, N_P2, 0)
                kept = slot if chunks == 8 else jnp.where(slot == Q2, P2, slot)
                return buf[kept, half, pl.ds(base + skip, take)].reshape(-1, 256)

            total = None
            for left, right in ((hi, hi), (hi, lo), (lo, hi)):
                term = lax.dot_general(load(left, rows, a), load(right, cols, b), (((0,), (0,)), ((), ())),
                                       preferred_element_type=jnp.float32)
                total = term if total is None else total + term
            total = total.reshape(4, 2, 32, 256)
            for k in range(2):
                strips = total[:, k]
                prod[k, start + t] = prod[k, start + t] + strips if skip else strips

    def core_copy(batch):
        span = pl.ds(FIRST[batch], COUNT[batch])
        return pltpu.make_async_remote_copy(
            src_ref=prod.at[1 - core, span], dst_ref=core_in.at[span],
            send_sem=core_send.at[batch], recv_sem=core_recv.at[batch],
            device_id=(at_grp(0, 0, 1), blk), device_id_type=MESH)

    def y_copy(batch, leg):
        first, count = FIRST[batch], COUNT[batch]
        if batch in DIRECT:
            leg_strip, leg_land = leg + 1, leg
            span = pl.ds(first, count)
            return pltpu.make_async_remote_copy(
                src_ref=prod.at[core, span, lax.rem(y + leg_strip, 4)], dst_ref=y_in.at[leg_land, span],
                send_sem=y_send.at[batch * 4 + leg], recv_sem=y_recv.at[batch * 4 + leg],
                device_id=(at_grp(0, leg_strip, 0), blk), device_id_type=MESH)
        first, count = [(first, count // 2), (first + count // 2, count - count // 2), (first, count), (first, count)][leg]
        strip, dy, land = [(2, 1, 0), (2, 3, 0), (1, 1, 1), (3, 3, 2)][leg]
        span = pl.ds(first, count)
        return pltpu.make_async_remote_copy(
            src_ref=prod.at[core, span, lax.rem(y + strip, 4)], dst_ref=y_in.at[land, span],
            send_sem=y_send.at[batch * 4 + leg], recv_sem=y_recv.at[batch * 4 + leg],
            device_id=(at_grp(0, dy, 0), blk), device_id_type=MESH)

    def y_begin(batch):
        if batch in DIRECT:
            y_copy(batch, 2).start()
        y_copy(batch, 0).start()
        y_copy(batch, 1).start()

    def y_turn(batch):
        first, count = FIRST[batch], COUNT[batch]
        if batch in DIRECT:
            return
        y_copy(batch, 0).wait()
        y_copy(batch, 1).wait()

        @pl.loop(first, first + count)
        def _(q):
            strip = jnp.where(q < first + count // 2, lax.rem(y + 1, 4), lax.rem(y + 3, 4))
            prod[core, q, strip] = prod[core, q, strip] + y_in[0, q]

        y_copy(batch, 2).start()
        y_copy(batch, 3).start()

    def core_finish(batch):
        core_copy(batch).wait()

        @pl.loop(FIRST[batch], FIRST[batch] + COUNT[batch])
        def _(q):
            prod[core, q] = prod[core, q] + core_in[q]

        y_begin(batch)

    def y_finish(batch):
        for leg in (0, 1, 2) if batch in DIRECT else (2, 3):
            y_copy(batch, leg).wait()

        @pl.loop(FIRST[batch], FIRST[batch] + COUNT[batch])
        def _(q):
            total = prod[core, q, y] + (y_in[1, q] + y_in[2, q])
            prod[core, q, y] = total + y_in[0, q] if batch in DIRECT else total

    facts = {}
    for tiles_of in BATCHES:
        for chunks, tiles in tiles_of:
            for s, _, u, _ in tiles:
                if (s, u) not in facts:
                    one, two = at_blk(*OFFSET[s]), at_blk(*OFFSET[u])
                    diff = lax.rem(one - two + 16, 16)
                    straight = diff <= 8
                    place = {8: 0, 5: 0, 3: 1, 4: lax.div(z, 4)}[chunks]
                    facts[s, u] = (straight, jnp.where(straight, two, one), jnp.where(straight, diff, 16 - diff) + 6 * place)

    def deliver(batch, wait=False):
        start = FIRST[batch]
        for chunks, tiles in BATCHES[batch]:
            for pair in dict.fromkeys((s, u) for s, _, u, _ in tiles):
                halves = [(i, j) for s, i, u, j in tiles if (s, u) == pair]
                straight, owner, slot = facts[pair]

                @pl.loop(0, len(halves))
                def _(t, halves=halves, straight=straight, owner=owner, slot=slot, start=start):
                    i, j = (pick(t, list(side)) for side in zip(*halves))
                    a, b = jnp.where(straight, i, j), jnp.where(straight, j, i)
                    src, sem = prod.at[core, start + t, y], slot * 4 + h * 2 + b
                    mine = jnp.logical_and(a == h, owner == blk)
                    if not wait:
                        @pl.when(mine)
                        def _():
                            pltpu.make_async_copy(src, fin.at[slot, h, b], fin_recv.at[sem]).start()

                    @pl.when(jnp.logical_not(mine))
                    def _():
                        copy = pltpu.make_async_remote_copy(
                            src_ref=src, dst_ref=fin.at[slot, h, b], send_sem=fin_send.at[start + t],
                            recv_sem=fin_recv.at[sem], device_id=(a * 8 + y * 2 + core, owner), device_id_type=MESH)
                        if wait:
                            copy.wait_send()
                        else:
                            copy.start()
                start += len(halves)

    def collect(distances):
        for d in distances:
            slots = [d, d + 6] if d in (3, 4, 5) else [d]
            for b in range(2):
                total = None
                for slot in slots:
                    for src in range(2):
                        pltpu.make_async_copy(fin.at[slot, src, b], fin.at[slot, src, b],
                                              fin_recv.at[slot * 4 + src * 2 + b]).wait()
                    term = fin[slot, 0, b] + fin[slot, 1, b]
                    total = term if total is None else total + term
                for c in range(2):
                    out[pl.ds(d * 128 + b * 2 + c, 32, stride=4), :] = total[:, c * 128:(c + 1) * 128]

    def pass_on(slot, then, half, pieces):
        for i in pieces:
            link(slot, half, i).wait_recv()
            link(then, half, i).start()

    def arrive(slot, half, pieces):
        for i in pieces:
            link(slot, half, i).wait_recv()

    def second_hops(half):
        for i in range(N_M2):
            if i < N_P2:
                link(P2, half, i).start()
            link(M2, half, i).start()

    multiply(0, 0)
    core_copy(0).start()
    pass_on(P1, Q1, 0, range(0, NEAR // 4))
    core_finish(0)
    pass_on(P1, Q1, 0, range(NEAR // 4, NEAR // 2))
    y_turn(0)
    pass_on(P1, Q1, 0, range(NEAR // 2, NEAR))
    arrive(M1, 0, range(NEAR))
    second_hops(0)
    split_near(P1, 0)
    split_near(M1, 0)
    multiply(1, 0)
    y_finish(0)
    deliver(0)
    pass_on(P1, Q1, 1, range(0, NEAR // 4))
    arrive(Q1, 0, range(NEAR))
    split_near(Q1, 0)
    multiply(1, 1)
    core_copy(1).start()
    pass_on(P1, Q1, 1, range(NEAR // 4, NEAR // 2))
    core_finish(1)
    pass_on(P1, Q1, 1, range(NEAR // 2, 3 * NEAR // 4))
    y_turn(1)
    pass_on(P1, Q1, 1, range(3 * NEAR // 4, NEAR))
    arrive(M1, 1, range(NEAR))
    second_hops(1)
    split_near(P1, 1)
    split_near(M1, 1)
    multiply(2, 0)
    core_copy(2).start()
    y_finish(1)
    deliver(1)
    pass_on(P2, Q2, 0, [0, 1])
    core_finish(2)
    arrive(Q1, 1, range(NEAR))
    split_near(Q1, 1)
    multiply(3, 0)
    core_copy(3).start()
    pass_on(P2, Q2, 0, [2, 3])
    y_turn(2)
    split_far(P2, 0)
    core_finish(3)
    arrive(M2, 0, range(N_M2))
    split_far(M2, 0)
    for group in range(3):
        multiply(4, group)
    core_copy(4).start()
    y_finish(2)
    y_turn(3)
    pass_on(P2, Q2, 1, [0])
    arrive(Q2, 0, range(N_P2))
    split_far(Q2, 0)
    for group in range(2):
        multiply(5, group)
    core_copy(5).start()
    core_finish(4)
    pass_on(P2, Q2, 1, [1])
    y_finish(3)
    core_finish(5)
    pass_on(P2, Q2, 1, [2])
    y_turn(4)
    y_turn(5)
    pass_on(P2, Q2, 1, [3])
    split_far(P2, 1)
    for group in range(2):
        multiply(6, group)
    core_copy(6).start()
    y_finish(4)
    arrive(M2, 1, range(N_P2))
    split_far(M2, 1, 0, N_P2)
    multiply(7, 0)
    core_copy(7).start()
    core_finish(6)
    multiply(8, 0, 0, N_P2)
    y_finish(5)
    core_finish(7)
    y_turn(6)
    deliver(2)
    deliver(3)
    arrive(M2, 1, range(N_P2, N_M2))
    split_far(M2, 1, N_P2)
    multiply(8, 0, N_P2, N_M2 - N_P2)
    core_copy(8).start()
    arrive(Q2, 1, range(N_P2))
    split_far(Q2, 1)
    for group in range(2):
        multiply(9, group)
    core_copy(9).start()
    deliver(4)
    y_turn(7)
    core_finish(8)
    deliver(5)
    core_finish(9)
    y_finish(6)
    deliver(6)
    y_turn(8)
    y_finish(7)
    deliver(7)
    y_turn(9)
    for half in range(2):
        for slot, n in ((P1, NEAR), (M1, NEAR), (Q1, NEAR), (M2, N_M2), (P2, N_P2), (Q2, N_P2)):
            for i in range(n):
                link(slot, half, i).wait_send()
    for batch in range(4):
        deliver(batch, wait=True)
    y_finish(8)
    deliver(8)
    collect([0, 1, 2, 6, 7, 8])
    for batch in range(4, 7):
        deliver(batch, wait=True)
    y_finish(9)
    deliver(9)
    for batch in range(7, len(BATCHES)):
        deliver(batch, wait=True)
    collect([3, 4, 5])


def per_device(factors):
    aux, orbitals, width = factors.shape
    chunk = aux // 8
    dma = pltpu.SemaphoreType.DMA
    n = len(BATCHES)
    out = pl.pallas_call(
        kernel,
        out_shape=jax.ShapeDtypeStruct((9 * 32 * 4, 128), jnp.float32),
        in_specs=[pl.BlockSpec(memory_space=pl.ANY)],
        out_specs=pl.BlockSpec(memory_space=pltpu.VMEM),
        scratch_shapes=[
            pltpu.VMEM((3, 2, aux, orbitals, 256), jnp.float32),
            pltpu.VMEM((2, N_M2, chunk, orbitals, 256), jnp.float32),
            pltpu.VMEM((2, N_P2, chunk, orbitals, 256), jnp.float32),
            pltpu.VMEM((2, N_P2, chunk, orbitals, 256), jnp.float32),
            pltpu.VMEM((aux, orbitals, 256), jnp.float32),
            pltpu.VMEM((6, 2, 8, chunk * orbitals, 256), jnp.bfloat16),
            pltpu.VMEM((6, 2, 8, chunk * orbitals, 256), jnp.bfloat16),
            pltpu.VMEM((2, TILES, 4, 32, 256), jnp.float32),
            pltpu.VMEM((TILES, 4, 32, 256), jnp.float32),
            pltpu.VMEM((3, TILES, 32, 256), jnp.float32),
            pltpu.VMEM((12, 2, 2, 32, 256), jnp.float32),
            dma((6 * NEAR + 26,)), dma((6 * NEAR + 26,)), dma, dma((n,)), dma((n,)), dma((4 * n,)), dma((4 * n,)), dma((TILES,)), dma((48,)),
        ],
        compiler_params=pltpu.CompilerParams(
            collective_id=0, has_side_effects=True, vmem_limit_bytes=62 * 2**20),
        cost_estimate=pl.CostEstimate(flops=6 * 9 * 512 * 512 * aux * orbitals, bytes_accessed=4 * 2**20,
                                      transcendentals=0),
        name="exchange",
    )(factors)
    return out.reshape(9, 32, 1, width)


def solution(mesh):
    return jax.shard_map(
        per_device,
        mesh=mesh,
        in_specs=(P("grp", None, "blk"),),
        out_specs=P(None, "grp", "blk", None),
        check_vma=False,
    )
```
